128 devices in a mesh: ty: 4 (over z), tx: 8 (over y_lo, x), mode: 4 (over y_hi, core).
Axes of the slice: x: 4, y: 4 (y_hi: 2, y_lo: 2; y = y_hi * 2 + y_lo), z: 4, core: 2. Of those that a mesh axis runs over, the one named last changes fastest.
Arguments:
- object_field: float32 [2, 2048, 2048], P(None, 'ty', 'tx')
- probe: float32 [2, 4, 512, 512], P(None, 'mode')
- amplitudes: float32 [32, 512, 512], P(('ty', 'tx')), may hold values from 0.2 to 1.5
- positions: int32 [32, 2], replicated, may hold values from 0 to 1920, as said below
- owned: int32 [32, 1], P(('ty', 'tx')), may hold values from 0 to 31, as said below
Outputs:
- object_new: float32 [2, 2048, 2048], P(None, 'ty', 'tx')
- probe_new: float32 [2, 4, 512, 512], P(None, 'mode')
The draws below stay inside these ranges and needn't reach their ends.
Inputs may be any that keep to these rules, and one draw needn't show every extreme that they name: Every position id appears exactly once in owned. Each centre has both coordinates a multiple of 128 and lies inside the tile that owns it; the positions of one tile differ.
All inputs are finite; a program needn't handle non-finite values.
Results may differ from the reference program's by a relative error of at most 0.0003.
Values sent between devices are 32-bit elements; how exact they have to be, the bound alone decides.
No kernel may reach another device: no remote copies, remote signals or barrier semaphores. Data moves between devices by JAX's collectives and lax.ppermute only.
A program may use at most 128 MiB of HBM per device.

```python
import math
import jax
import jax.numpy as jnp
from jax import lax

PR = 512
STEP = 128
TW = 256
TH = 512
POS_TILE = 1
ITERS = 2
MODES = 4
TILES = 32
NPOS = 32
NY = 2048
NX = 2048


def scan_layout(key):
    key_order, key_slots = jax.random.split(key)
    across = NX // TW
    slot_cols = TW // STEP
    slot_total = TH // STEP * slot_cols
    owned_ids = jax.random.permutation(key_order, NPOS).astype(jnp.int32).reshape(TILES, POS_TILE)
    scores = jax.random.randint(key_slots, (TILES, slot_total), 0, 1 << 20, dtype=jnp.int32) * slot_total
    slot_ids = jnp.arange(slot_total, dtype=jnp.int32)
    scores = scores + slot_ids[None, :]
    tile_ids = jnp.arange(TILES, dtype=jnp.int32)
    first_corner = (tile_ids[:, None] == 0) & (slot_ids[None, :] == 0)
    last_corner = (tile_ids[:, None] == TILES - 1) & (slot_ids[None, :] == slot_total - 1)
    scores = jnp.where(first_corner | last_corner, jnp.int32(-1), scores)
    chosen = jnp.argsort(scores, axis=1, stable=True)[:, :POS_TILE].astype(jnp.int32)
    rows_at = (tile_ids // across)[:, None] * TH + chosen // slot_cols * STEP
    cols_at = (tile_ids % across)[:, None] * TW + chosen % slot_cols * STEP
    centres = jnp.stack([rows_at, cols_at], axis=-1).reshape(NPOS, 2)
    placed = jnp.zeros((NPOS, 2), jnp.int32).at[owned_ids.reshape(-1)].set(centres)
    return (owned_ids, placed)


def draw_owned(key, part):
    owned_ids, placed = scan_layout(key)
    return owned_ids


def draw_positions(key, part):
    owned_ids, placed = scan_layout(key)
    return placed


def draw_object_field(key, part):
    key = jax.random.fold_in(key, 7)
    key_rough, key_phase = jax.random.split(key)
    ramp = 0.65 + 0.55 * jnp.arange(NX, dtype=jnp.float32)[None, :] / max(NX - 1, 1) * jnp.ones((NY, 1), jnp.float32)
    rough = jax.random.uniform(key_rough, (NY, NX), jnp.float32, 0.6, 1.4)
    phases = jax.random.uniform(key_phase, (NY, NX), jnp.float32, -math.pi, math.pi)
    magnitude = ramp * rough
    return jnp.stack([magnitude * jnp.cos(phases), magnitude * jnp.sin(phases)])


def draw_probe(key, part):
    key = jax.random.fold_in(key, 9)
    exponents = jnp.arange(MODES, dtype=jnp.float32) / max(MODES - 1, 1)
    levels = jnp.exp(-0.5 * math.log(3.0) * exponents)
    values = jax.random.normal(key, (2, MODES, PR, PR), jnp.float32)
    return values * levels[None, :, None, None] * math.sqrt(0.5)


def block_levels(stream_key, dims, cuts, low, largest):
    def one(position, shards_of):
        draws = jax.random.uniform(jax.random.fold_in(jax.random.fold_in(stream_key, 6), position), (shards_of,), jnp.float32, low / len(cuts), largest / len(cuts))
        return jnp.repeat(jnp.exp(draws), dims[position] // shards_of).reshape((-1,) + (1,) * (len(dims) - position - 1))

    factor_of = one(*cuts[0])
    for cut in cuts[1:]:
        factor_of = factor_of * one(*cut)
    return factor_of


def setup_inputs(seed: int = 0) -> dict:
    splits = jax.random.split(jax.random.key(seed), 6)
    object_field = draw_object_field(jax.random.fold_in(splits[5], 71), 0)
    probe = draw_probe(jax.random.fold_in(splits[5], 71), 0)
    amplitudes = jnp.clip(0.2 + 1.3 * jax.random.uniform(splits[2], (NPOS, PR, PR), jnp.float32) ** block_levels(splits[2], (NPOS, PR, PR), ((0, 32),), -0.2, 0.2), 0.2, 1.5)
    positions = draw_positions(jax.random.fold_in(splits[5], 71), 0)
    owned = draw_owned(jax.random.fold_in(splits[5], 71), 0)
    return dict(object_field=object_field, probe=probe, amplitudes=amplitudes, positions=positions, owned=owned)


def tables(points):
    indices = jnp.arange(points, dtype=jnp.int32)
    product = indices[:, None] * indices[None, :] % points
    angles = product.astype(jnp.float32) * (2.0 * math.pi / points)
    factor = 1.0 / math.sqrt(points)
    return (jnp.cos(angles) * factor, jnp.sin(angles) * factor)

def apply_left(matrix, values):
    return jnp.einsum('ku,...uv->...kv', matrix, values, precision=lax.Precision.HIGHEST)

def apply_right(values, matrix):
    return jnp.einsum('...uv,vl->...ul', values, matrix, precision=lax.Precision.HIGHEST)

def transform(real_part, imag_part, cosine, sine_table, direction_sign):
    first_real = apply_left(cosine, real_part) - direction_sign * apply_left(sine_table, imag_part)
    first_imag = apply_left(cosine, imag_part) + direction_sign * apply_left(sine_table, real_part)
    second_real = apply_right(first_real, cosine) - direction_sign * apply_right(first_imag, sine_table)
    second_imag = apply_right(first_imag, cosine) + direction_sign * apply_right(first_real, sine_table)
    return (second_real, second_imag)

def iterate(field, modes, amplitudes, positions, owned_ids):
    half_width = PR // 2
    rows_all = field.shape[1]
    cols_all = field.shape[2]
    padded = jnp.pad(field, ((0, 0), (half_width, half_width), (half_width, half_width)))
    cosine, sine_table = tables(PR)
    mode_real = modes[0]
    mode_imag = modes[1]

    def visit(carry, entry):
        grad_pad, probe_grad, power = carry
        which, measured = entry
        zero_index = jnp.zeros((), jnp.int32)
        row_start = positions[which, 0].astype(jnp.int32)
        col_start = positions[which, 1].astype(jnp.int32)
        anchor = (zero_index, row_start, col_start)
        window = lax.dynamic_slice(padded, anchor, (2, PR, PR))
        window_real = window[0]
        window_imag = window[1]
        exit_real = mode_real * window_real - mode_imag * window_imag
        exit_imag = mode_real * window_imag + mode_imag * window_real
        far_real, far_imag = transform(exit_real, exit_imag, cosine, sine_table, -1.0)
        intensity = lax.optimization_barrier(jnp.sum(far_real * far_real + far_imag * far_imag, axis=0))
        weight = 1.0 - measured / jnp.maximum(jnp.sqrt(intensity), 1.0)
        back_real, back_imag = transform(weight * far_real, weight * far_imag, cosine, sine_table, 1.0)
        grad_real = lax.optimization_barrier(jnp.sum(mode_real * back_real + mode_imag * back_imag, axis=0))
        grad_imag = lax.optimization_barrier(jnp.sum(mode_real * back_imag - mode_imag * back_real, axis=0))
        piece = lax.dynamic_slice(grad_pad, anchor, (2, PR, PR)) + jnp.stack([grad_real, grad_imag])
        grad_pad = lax.dynamic_update_slice(grad_pad, piece, anchor)
        probe_real = window_real * back_real + window_imag * back_imag
        probe_imag = window_real * back_imag - window_imag * back_real
        probe_grad = probe_grad + jnp.stack([probe_real, probe_imag])
        power = power + jnp.mean(window_real * window_real + window_imag * window_imag)
        return ((grad_pad, probe_grad, power), None)
    start_state = (jnp.zeros(padded.shape, jnp.float32), jnp.zeros(modes.shape, jnp.float32), jnp.zeros((), jnp.float32))
    (grad_pad, probe_grad, power), unused = lax.scan(visit, start_state, (owned_ids, amplitudes))
    object_grad = grad_pad[:, half_width:half_width + rows_all, half_width:half_width + cols_all]
    probe_power = jnp.sum(lax.optimization_barrier(jnp.mean(mode_real * mode_real + mode_imag * mode_imag, axis=(1, 2))))
    coverage = amplitudes.shape[0] * PR * PR / (rows_all * cols_all)
    illumination = probe_power * coverage
    return (field - object_grad / illumination, modes - probe_grad / power)

def reference(object_field, probe, amplitudes, positions, owned):
    owned_ids = owned.reshape(-1).astype(jnp.int32)
    field = object_field
    modes = probe
    for iteration in range(ITERS):
        field, modes = iterate(field, modes, amplitudes, positions, owned_ids)
    return (field, modes)
```

```python
import functools

import jax
import jax.numpy as jnp
import numpy as np
from jax import lax
from jax.experimental import pallas as pl
from jax.experimental.pallas import tpu as pltpu
from jax.sharding import PartitionSpec as P

PR = 512
HALF = 256
F32 = jnp.float32
BF16 = jnp.bfloat16
MIB = 1 << 20

ROW, COL, ROW_LEFT, ROW_RIGHT, X, Z, YL, YH, CORE = range(9)


def split_np(matrix):
    high = matrix.astype(jnp.bfloat16)
    low = (matrix - high.astype(np.float64)).astype(jnp.bfloat16)
    return high, low


def tables():
    k = np.arange(HALF)[:, None]
    u = np.arange(HALF)[None, :]
    out = []
    for odd in (0, 1):
        angle = 2.0 * np.pi * (((2 * k + odd) * u) % PR) / PR
        c, s = np.cos(angle) / np.sqrt(PR), np.sin(angle) / np.sqrt(PR)
        out.append(np.block([[c, s], [-s, c]]))
    even, odd = out
    parts = []
    for m in (even, odd, even.T, odd.T):
        parts.extend(split_np(np.ascontiguousarray(m)))
    return parts


def split(x):
    high = x.astype(BF16)
    return high, (x - high.astype(F32)).astype(BF16)


def dot(a, b):
    return jnp.dot(a, b, preferred_element_type=F32)


def left(mh, ml, x):
    xh, xl = split(x)
    return dot(mh[...], xh) + (dot(mh[...], xl) + dot(ml[...], xh))


def right(x, mh, ml):
    xh, xl = split(x)
    return dot(xh, mh[...]) + (dot(xl, mh[...]) + dot(xh, ml[...]))


def smem():
    return pl.BlockSpec(memory_space=pltpu.SMEM)


def vmem():
    return pl.BlockSpec(memory_space=pltpu.VMEM)


def call(kernel, sc, ins, outs, scratch=(), limit=32, flops=0):
    return pl.pallas_call(
        kernel,
        out_shape=[jax.ShapeDtypeStruct(s, F32) for s in outs],
        in_specs=[smem()] + [vmem()] * len(ins),
        out_specs=[vmem()] * len(outs),
        scratch_shapes=[pltpu.VMEM(s, F32) for s in scratch],
        compiler_params=pltpu.CompilerParams(vmem_limit_bytes=limit * MIB),
        cost_estimate=pl.CostEstimate(
            flops=flops,
            bytes_accessed=4 * sum(int(np.prod(s)) for s in outs) + sum(a.nbytes for a in ins),
            transcendentals=0,
        ),
    )(sc, *ins)


def at(start, size, unit):
    return pl.ds(pl.multiple_of(start * unit, unit), size)


def exact_parts(x):
    a = x.astype(BF16)
    rest = x - a.astype(F32)
    b = rest.astype(BF16)
    return a, b, (rest - b.astype(F32)).astype(BF16)


def order_kernel(sc, amp, out):
    core = sc[CORE]
    row = lax.broadcasted_iota(jnp.int32, (HALF, PR), 0)
    col = lax.broadcasted_iota(jnp.int32, (HALF, PR), 1)
    pick = jnp.where(col == 2 * row + core, 1.0, 0.0).astype(BF16)
    a, b, c = exact_parts(amp[...])
    rows = (dot(pick, a) + dot(pick, b)) + dot(pick, c)
    src = lax.broadcasted_iota(jnp.int32, (PR, PR), 0)
    dst = lax.broadcasted_iota(jnp.int32, (PR, PR), 1)
    want = jnp.where(dst < HALF, 2 * dst, 2 * (dst - HALF) + 1)
    move = jnp.where(src == want, 1.0, 0.0).astype(BF16)
    a, b, c = exact_parts(rows)
    out[...] = (dot(a, move) + dot(b, move)) + dot(c, move)


def strips_kernel(b, sc, up, own, down, mid, to_right, to_left, strip):
    strip[0 : 2 * b] = up[...]
    strip[2 * b : 6 * b] = own[...]
    strip[6 * b : 7 * b] = down[...]
    mid[...] = strip[at(sc[ROW], 4 * b, b)]
    to_right[...] = strip[at(sc[ROW_RIGHT], 4 * b, b)]
    to_left[...] = strip[at(sc[ROW_LEFT], 4 * b, b), 0:128]


def strips(b, sc, up, own, down):
    return call(
        functools.partial(strips_kernel, b),
        sc,
        (up, own, down),
        ((4 * b, 256), (4 * b, 256), (4 * b, 128)),
        scratch=((7 * b, 256),),
    )


def widen_kernel(sc, lft, mid, rgt, out):
    @pl.when(sc[COL] == 0)
    def _():
        out[:, 0:256] = lft[...]
        out[:, 256:512] = mid[...]

    @pl.when(sc[COL] != 0)
    def _():
        out[:, 0:128] = lft[:, 128:256]
        out[:, 128:384] = mid[...]
        out[:, 384:512] = rgt[...]


def widen(sc, lft, mid, rgt):
    return call(widen_kernel, sc, (lft, mid, rgt), ((mid.shape[0], PR),))[0]


def forward_tail(sc, w, p, tabs, far, keep, send, mid):
    meh, mel, moh, mol, teh, tel, toh, tol = tabs
    wr, wi = w[0], w[1]
    pr, pi = p[0], p[1]
    er = pr * wr - pi * wi
    ei = pr * wi + pi * wr
    total = jnp.concatenate([er[:HALF] + er[HALF:], ei[:HALF] + ei[HALF:]], axis=0)
    mid[0] = left(meh, mel, total)
    total = jnp.concatenate([er[:HALF] - er[HALF:], ei[:HALF] - ei[HALF:]], axis=0)
    mid[1] = left(moh, mol, total)
    core = sc[CORE]
    power = (jnp.sum(pr * pr) + jnp.sum(pi * pi)) * (1.0 / (PR * PR))
    for parity in (0, 1):
        rows = slice(parity * HALF, parity * HALF + HALF)
        yr, yi = mid[parity, 0:HALF], mid[parity, HALF:PR]
        total = jnp.concatenate([yr[:, :HALF] + yr[:, HALF:], yi[:, :HALF] + yi[:, HALF:]], axis=1)
        even = right(total, teh, tel)
        total = jnp.concatenate([yr[:, :HALF] - yr[:, HALF:], yi[:, :HALF] - yi[:, HALF:]], axis=1)
        odd = right(total, toh, tol)
        fr = jnp.concatenate([even[:, :HALF], odd[:, :HALF]], axis=1)
        fi = jnp.concatenate([even[:, HALF:], odd[:, HALF:]], axis=1)
        far[0, rows] = fr
        far[1, rows] = fi
        own = fr * fr + fi * fi

        @pl.when(core == parity)
        def _():
            keep[0:HALF] = own

        @pl.when(core != parity)
        def _():
            send[0:HALF] = own

    keep[HALF : HALF + 8] = jnp.full((8, PR), power, F32)
    send[HALF : HALF + 8] = jnp.full((8, PR), power, F32)


def forward_first_kernel(sc, mine, other, p, *rest):
    tabs, (w, far, keep, send, mid) = rest[:8], rest[8:]
    core = sc[CORE]
    w[core] = mine[...]
    w[1 - core] = other[...]
    forward_tail(sc, w, p, tabs, far, keep, send, mid)


def forward_second_kernel(sc, *rest):
    pieces, parts, tabs, (w, p, far, keep, send, mid) = rest[:4], rest[4:12], rest[12:20], rest[20:]
    core, yh, x, z = sc[CORE], sc[YH], sc[X], sc[Z]
    for which, piece in enumerate(pieces):
        plane = core if which < 2 else 1 - core
        parity = yh if which % 2 == 0 else 1 - yh
        for block in range(4):
            w[plane, at(2 * block + parity, 64, 64)] = piece[block * 64 : block * 64 + 64]
    for d in range(4):
        p[0, at(lax.rem(x + 4 - d, 4), 128, 128)] = parts[d][...]
        p[1, at(lax.rem(z + 4 - d, 4), 128, 128)] = parts[4 + d][...]
    forward_tail(sc, w, p, tabs, far, keep, send, mid)


FLOPS = 3 * 8 * PR**3
FIELD = (2, PR, PR)
EXT = (HALF + 8, PR)


def forward_first(sc, mine, other, p, tabs):
    return call(
        forward_first_kernel,
        sc,
        (mine, other, p, *tabs),
        (FIELD, FIELD, EXT, EXT),
        scratch=(FIELD,),
        limit=48,
        flops=FLOPS,
    )


def forward_second(sc, pieces, parts, tabs):
    return call(
        forward_second_kernel,
        sc,
        (*pieces, *parts, *tabs),
        (FIELD, FIELD, FIELD, EXT, EXT),
        scratch=(FIELD,),
        limit=48,
        flops=FLOPS,
    )


def inverse_kernel(sc, w, p, far, mine, other, *rest):
    tabs, outs = rest[:8], rest[8:]
    keep, send = outs[:2]
    part_a, part_b = outs[2:6], outs[6:10]
    mid, grad, weight = outs[10:]
    meh, mel, moh, mol, teh, tel, toh, tol = tabs
    core, x, z = sc[CORE], sc[X], sc[Z]
    weight[core] = mine[...]
    weight[1 - core] = other[...]
    for parity in (0, 1):
        rows = slice(parity * HALF, parity * HALF + HALF)
        yr = far[0, rows] * weight[parity]
        yi = far[1, rows] * weight[parity]
        even = right(jnp.concatenate([yr[:, :HALF], yi[:, :HALF]], axis=1), meh, mel)
        odd = right(jnp.concatenate([yr[:, HALF:], yi[:, HALF:]], axis=1), moh, mol)
        total = even + odd
        diff = even - odd
        mid[parity, 0:HALF] = jnp.concatenate([total[:, :HALF], diff[:, :HALF]], axis=1)
        mid[parity, HALF:PR] = jnp.concatenate([total[:, HALF:], diff[:, HALF:]], axis=1)
    even = left(teh, tel, mid[0])
    odd = left(toh, tol, mid[1])
    for top in (0, 1):
        rows = slice(top * HALF, top * HALF + HALF)
        chi = even - odd if top else even + odd
        cr, ci = chi[:HALF], chi[HALF:]
        pr, pi = p[0, rows], p[1, rows]
        gr = pr * cr + pi * ci
        gi = pr * ci - pi * cr

        @pl.when(core == 0)
        def _():
            keep[rows] = gr
            send[rows] = gi

        @pl.when(core != 0)
        def _():
            keep[rows] = gi
            send[rows] = gr

        wr, wi = w[0, rows], w[1, rows]
        grad[0, rows] = wr * cr + wi * ci
        grad[1, rows] = wr * ci - wi * cr
    power = (jnp.sum(w[0] * w[0]) + jnp.sum(w[1] * w[1])) * (1.0 / (PR * PR))
    for d in range(4):
        part_a[d][0:128] = grad[0, at(lax.rem(x + d, 4), 128, 128)]
        part_a[d][128:136] = jnp.full((8, PR), power, F32)
        part_b[d][...] = grad[1, at(lax.rem(z + d, 4), 128, 128)]


def inverse(sc, w, p, far, mine, other, tabs):
    outs = call(
        inverse_kernel,
        sc,
        (w, p, far, mine, other, *tabs),
        ((PR, PR), (PR, PR)) + ((136, PR),) * 4 + ((128, PR),) * 4,
        scratch=(FIELD, FIELD, (2, HALF, PR)),
        limit=48,
        flops=FLOPS,
    )
    return outs[0], outs[1], outs[2:6], outs[6:10]


def halve_kernel(sc, keep, got, stay, go):
    yh = sc[YH]
    for block in range(4):
        rows = slice(block * 64, block * 64 + 64)
        here = at(2 * block + yh, 64, 64)
        there = at(2 * block + 1 - yh, 64, 64)
        stay[rows] = keep[here] + got[here]
        go[rows] = keep[there] + got[there]


def fold_cols_kernel(sc, stay, got, lft, mid, rgt):
    g = stay[...] + got[...]

    @pl.when(sc[COL] == 0)
    def _():
        lft[...] = g[:, 0:256]
        mid[...] = g[:, 256:512]
        rgt[...] = jnp.zeros(rgt.shape, F32)

    @pl.when(sc[COL] != 0)
    def _():
        lft[:, 0:128] = jnp.zeros((g.shape[0], 128), F32)
        lft[:, 128:256] = g[:, 0:128]
        mid[...] = g[:, 128:384]
        rgt[...] = g[:, 384:512]


def fold_rows_kernel(sc, mid, from_right, from_left, up, own, down, strip):
    strip[...] = jnp.zeros(strip.shape, F32)
    strip[at(sc[ROW], 256, 64)] = mid[...]
    rows = at(sc[ROW_RIGHT], 256, 64)
    strip[rows] = strip[rows] + from_right[...]
    rows = at(sc[ROW_LEFT], 256, 64)
    strip[rows, 0:128] = strip[rows, 0:128] + from_left[...]
    up[...] = strip[0:128]
    own[...] = strip[128:384]
    down[...] = strip[384:448]


def update_kernel(sc, old, own, from_below, from_above, power, new, to_below, to_above):
    scale = 1.0 / (2.0 * power[0:1, 0:1])
    for block in range(4):
        rows = slice(block * 64, block * 64 + 64)
        g = own[rows]
        if block == 0:
            g = g + from_above[...]
        if block >= 2:
            g = g + from_below[(block - 2) * 64 : (block - 1) * 64]
        value = old[rows] - g * scale
        new[rows] = value
        if block >= 2:
            to_below[(block - 2) * 64 : (block - 1) * 64] = value
        if block == 0:
            to_above[...] = value


def join_kernel(sc, aa, ab, ba, bb, out):
    core, yh = sc[CORE], sc[YH]
    for block in range(4):
        rows = slice(block * 64, block * 64 + 64)
        out[core, at(2 * block + yh, 64, 64)] = aa[rows]
        out[core, at(2 * block + 1 - yh, 64, 64)] = ab[rows]
        out[1 - core, at(2 * block + yh, 64, 64)] = ba[rows]
        out[1 - core, at(2 * block + 1 - yh, 64, 64)] = bb[rows]


def scatter_rows_kernel(sc, a0, a1, a2, a3, b0, b1, b2, b3, *rest):
    out_a, out_b, (sum_a, sum_b) = rest[:4], rest[4:8], rest[8:]
    sum_a[...] = (a0[...] + a1[...]) + (a2[...] + a3[...])
    sum_b[...] = (b0[...] + b1[...]) + (b2[...] + b3[...])
    for d in range(4):
        out_a[d][0:32] = sum_a[at(lax.rem(sc[Z] + d, 4), 32, 32)]
        out_a[d][32:40] = sum_a[128:136]
        out_b[d][...] = sum_b[at(lax.rem(sc[X] + d, 4), 32, 32)]


def scatter_pair_kernel(sc, a0, a1, a2, a3, b0, b1, b2, b3, stay, go, sum_a, sum_b):
    sum_a[...] = (a0[...] + a1[...]) + (a2[...] + a3[...])
    sum_b[...] = (b0[...] + b1[...]) + (b2[...] + b3[...])
    yl = sc[YL]
    for out, half in ((stay, yl), (go, 1 - yl)):
        out[0:16] = sum_a[at(half, 16, 16)]
        out[16:32] = sum_b[at(half, 16, 16)]
        out[32:40] = sum_a[32:40]


def probe_shard_kernel(sc, p, stay, got, out):
    x, z, yl = sc[X], sc[Z], sc[YL]
    total = stay[...] + got[...]
    scale = 1.0 / total[32:33, 0:1]
    out[0:16] = p[0, at(8 * x + 2 * z + yl, 16, 16)] - total[0:16] * scale
    out[16:32] = p[1, at(8 * z + 2 * x + yl, 16, 16)] - total[16:32] * scale


def gather_pair_kernel(sc, mine, other, out_a, out_b):
    yl = sc[YL]
    for half, src in ((yl, mine), (1 - yl, other)):
        out_a[at(half, 16, 16)] = src[0:16]
        out_b[at(half, 16, 16)] = src[16:32]


def gather_rows_kernel(sc, a0, a1, a2, a3, b0, b1, b2, b3, out_a, out_b):
    for d, (a, b) in enumerate(((a0, b0), (a1, b1), (a2, b2), (a3, b3))):
        out_a[at(lax.rem(sc[Z] + 4 - d, 4), 32, 32)] = a[...]
        out_b[at(lax.rem(sc[X] + 4 - d, 4), 32, 32)] = b[...]


def gather_all_kernel(sc, a0, a1, a2, a3, b0, b1, b2, b3, out):
    for d, (a, b) in enumerate(((a0, b0), (a1, b1), (a2, b2), (a3, b3))):
        out[0, at(lax.rem(sc[X] + 4 - d, 4), 128, 128)] = a[...]
        out[1, at(lax.rem(sc[Z] + 4 - d, 4), 128, 128)] = b[...]


def swap_core(v):
    return lax.ppermute(v, "mode", [(0, 1), (1, 0), (2, 3), (3, 2)])


def swap_plane(v):
    return lax.ppermute(v, "mode", [(0, 2), (2, 0), (1, 3), (3, 1)])


def swap_y(v):
    return lax.ppermute(v, "tx", [(i, (i + 4) % 8) for i in range(8)])


def ring_x(v, d):
    return lax.ppermute(v, "tx", [(4 * y + i, 4 * y + (i + d) % 4) for y in range(2) for i in range(4)])


def ring_z(v, d):
    return lax.ppermute(v, "ty", [(i, (i + d) % 4) for i in range(4)])


def step(v, axis, d):
    count = {"ty": 4, "tx": 8}[axis]
    return lax.ppermute(v, axis, [(i, i + d) for i in range(count) if 0 <= i + d < count])


def reduce_probe(sc, p, part_a, part_b):
    got_a = [part_a[0]] + [ring_x(part_a[d], d) for d in (1, 3, 2)]
    got_b = [part_b[0]] + [ring_z(part_b[d], d) for d in (1, 3, 2)]
    outs = call(
        scatter_rows_kernel,
        sc,
        (*got_a, *got_b),
        ((40, PR),) * 4 + ((32, PR),) * 4,
        scratch=((136, PR), (128, PR)),
    )
    got_a = [outs[0]] + [ring_z(outs[d], d) for d in (1, 3, 2)]
    got_b = [outs[4]] + [ring_x(outs[4 + d], d) for d in (1, 3, 2)]
    stay, go = call(
        scatter_pair_kernel,
        sc,
        (*got_a, *got_b),
        ((40, PR), (40, PR)),
        scratch=((40, PR), (32, PR)),
    )
    shard = call(probe_shard_kernel, sc, (p, stay, swap_y(go)), ((32, PR),))[0]
    a, b = call(gather_pair_kernel, sc, (shard, swap_y(shard)), ((32, PR), (32, PR)))
    parts_a = [a] + [ring_z(a, d) for d in (1, 2, 3)]
    parts_b = [b] + [ring_x(b, d) for d in (1, 2, 3)]
    a, b = call(gather_rows_kernel, sc, (*parts_a, *parts_b), ((128, PR), (128, PR)))
    parts_a = [a] + [ring_x(a, d) for d in (1, 2, 3)]
    parts_b = [b] + [ring_z(b, d) for d in (1, 2, 3)]
    return (*parts_a, *parts_b)


def window_sides(b, sc, own, to_below, to_above):
    up = step(to_below, "ty", 1)
    down = step(to_above, "ty", -1)
    mid, to_right, to_left = strips(b, sc, up, own, down)
    lft = step(to_right, "tx", 1)
    rgt = step(to_left, "tx", -1)
    return widen(sc, lft, mid, rgt)


def fold_gradient(sc, old, keep, send, power):
    stay, go = call(halve_kernel, sc, (keep, swap_core(send)), ((HALF, PR), (HALF, PR)))
    lft, mid, rgt = call(
        fold_cols_kernel,
        sc,
        (stay, swap_plane(go)),
        ((HALF, 256), (HALF, 256), (HALF, 128)),
    )
    up, own, down = call(
        fold_rows_kernel,
        sc,
        (mid, step(lft, "tx", -1), step(rgt, "tx", 1)),
        ((128, 256), (256, 256), (64, 256)),
        scratch=((448, 256),),
    )
    return call(
        update_kernel,
        sc,
        (old, own, step(up, "ty", -1), step(down, "ty", 1), power),
        ((256, 256), (128, 256), (64, 256)),
    )


def weights(amp, keep, send):
    half = keep + swap_core(send)
    total = half + swap_plane(half)
    mine = 1.0 - amp / jnp.maximum(jnp.sqrt(total[:HALF]), 1.0)
    return mine, swap_core(mine), total[HALF:]


def body(object_field, probe, amplitudes, positions, owned):
    ty, tx, mode = lax.axis_index("ty"), lax.axis_index("tx"), lax.axis_index("mode")
    tile = ty * 8 + tx
    tiles = positions[:, 0] // 512 * 8 + positions[:, 1] // 256
    row_blocks = positions[:, 0] % 512 // 128
    col_blocks = positions[:, 1] % 256 // 128

    def pick(values, which):
        return jnp.sum(jnp.where(tiles == which, values, 0))

    core = mode % 2
    sc = jnp.stack(
        [
            pick(row_blocks, tile),
            pick(col_blocks, tile),
            pick(row_blocks, tile - 1),
            pick(row_blocks, tile + 1),
            tx % 4,
            ty,
            tx // 4,
            mode // 2,
            core,
        ]
    ).astype(jnp.int32)
    tabs = [jnp.asarray(t) for t in tables()]
    p = probe[:, 0]
    amp = call(order_kernel, sc, (amplitudes[0],), ((HALF, PR),), limit=48)[0]

    plane = lax.dynamic_index_in_dim(object_field, core, 0, keepdims=False)
    quarter = lax.dynamic_index_in_dim(plane.reshape(4, 2, 64, 256), mode // 2, 1, keepdims=False)
    quarter = quarter.reshape(256, 256)
    mine = window_sides(128, sc, plane, plane[256:512], plane[0:128])
    w, far, keep, send = forward_first(sc, mine, swap_core(mine), p, tabs)
    weight, weight_other, power = weights(amp, keep, send)
    keep, send, part_a, part_b = inverse(sc, w, p, far, weight, weight_other, tabs)
    new, to_below, to_above = fold_gradient(sc, quarter, keep, send, power)
    parts = reduce_probe(sc, p, part_a, part_b)

    aa = window_sides(64, sc, new, to_below, to_above)
    ab = swap_plane(aa)
    pieces = (aa, ab, swap_core(aa), swap_core(ab))
    w, p, far, keep, send = forward_second(sc, pieces, parts, tabs)
    weight, weight_other, power = weights(amp, keep, send)
    keep, send, part_a, part_b = inverse(sc, w, p, far, weight, weight_other, tabs)
    aa = fold_gradient(sc, new, keep, send, power)[0]
    parts = reduce_probe(sc, p, part_a, part_b)
    ab = swap_plane(aa)
    pieces = (aa, ab, swap_core(aa), swap_core(ab))
    out_field = call(join_kernel, sc, pieces, ((2, 512, 256),))[0]
    out_probe = call(gather_all_kernel, sc, parts, (FIELD,))[0]
    return out_field, out_probe[:, None]


def solution(mesh):
    placed = (
        P(None, "ty", "tx"),
        P(None, "mode", None, None),
        P(("ty", "tx"), None, None),
        P(),
        P(("ty", "tx"), None),
    )
    return jax.shard_map(
        body,
        mesh=mesh,
        in_specs=placed,
        out_specs=(P(None, "ty", "tx"), P(None, "mode", None, None)),
        check_vma=False,
    )
```

```python
import functools

import jax
import jax.numpy as jnp
import numpy as np
from jax import lax
from jax.experimental import pallas as pl
from jax.experimental.pallas import tpu as pltpu
from jax.sharding import PartitionSpec as P

PR = 512
HALF = 256
F32 = jnp.float32
BF16 = jnp.bfloat16
MIB = 1 << 20

ROW, COL, ROW_LEFT, ROW_RIGHT, X, Z, YL, YH, CORE = range(9)


def split_np(matrix):
    high = matrix.astype(jnp.bfloat16)
    low = (matrix - high.astype(np.float64)).astype(jnp.bfloat16)
    return high, low


def tables():
    k = np.arange(HALF)[:, None]
    u = np.arange(HALF)[None, :]
    out = []
    for odd in (0, 1):
        angle = 2.0 * np.pi * (((2 * k + odd) * u) % PR) / PR
        c, s = np.cos(angle) / np.sqrt(PR), np.sin(angle) / np.sqrt(PR)
        out.append(np.block([[c, s], [-s, c]]))
    even, odd = out
    parts = []
    for m in (even, odd, even.T, odd.T):
        parts.extend(split_np(np.ascontiguousarray(m)))
    return parts


def split(x):
    high = x.astype(BF16)
    return high, (x - high.astype(F32)).astype(BF16)


def dot(a, b):
    return jnp.dot(a, b, preferred_element_type=F32)


def left(mh, ml, x):
    xh, xl = split(x)
    return dot(mh[...], xh) + (dot(mh[...], xl) + dot(ml[...], xh))


def right(x, mh, ml):
    xh, xl = split(x)
    return dot(xh, mh[...]) + (dot(xl, mh[...]) + dot(xh, ml[...]))


def smem():
    return pl.BlockSpec(memory_space=pltpu.SMEM)


def vmem():
    return pl.BlockSpec(memory_space=pltpu.VMEM)


def call(kernel, sc, ins, outs, scratch=(), limit=6, flops=0):
    return pl.pallas_call(
        kernel,
        out_shape=[jax.ShapeDtypeStruct(s, F32) for s in outs],
        in_specs=[smem()] + [vmem()] * len(ins),
        out_specs=[vmem()] * len(outs),
        scratch_shapes=[pltpu.VMEM(s, F32) for s in scratch],
        compiler_params=pltpu.CompilerParams(vmem_limit_bytes=limit * MIB),
        cost_estimate=pl.CostEstimate(
            flops=flops,
            bytes_accessed=4 * sum(int(np.prod(s)) for s in outs) + sum(a.nbytes for a in ins),
            transcendentals=0,
        ),
    )(sc, *ins)


def at(start, size, unit):
    return pl.ds(pl.multiple_of(start * unit, unit), size)


def exact_parts(x):
    a = x.astype(BF16)
    rest = x - a.astype(F32)
    b = rest.astype(BF16)
    return a, b, (rest - b.astype(F32)).astype(BF16)


def order_kernel(sc, amp, out):
    core = sc[CORE]
    row = lax.broadcasted_iota(jnp.int32, (HALF, PR), 0)
    col = lax.broadcasted_iota(jnp.int32, (HALF, PR), 1)
    pick = jnp.where(col == 2 * row + core, 1.0, 0.0).astype(BF16)
    a, b, c = exact_parts(amp[...])
    rows = (dot(pick, a) + dot(pick, b)) + dot(pick, c)
    src = lax.broadcasted_iota(jnp.int32, (PR, PR), 0)
    dst = lax.broadcasted_iota(jnp.int32, (PR, PR), 1)
    want = jnp.where(dst < HALF, 2 * dst, 2 * (dst - HALF) + 1)
    move = jnp.where(src == want, 1.0, 0.0).astype(BF16)
    a, b, c = exact_parts(rows)
    out[...] = (dot(a, move) + dot(b, move)) + dot(c, move)


def first_strips_kernel(sc, up, own, down, mid, to_right, to_left, kept, strip):
    strip[0:256] = up[...]
    strip[256:768] = own[...]
    strip[768:896] = down[...]
    mid[...] = strip[at(sc[ROW], 512, 128)]
    to_right[...] = strip[at(sc[ROW_RIGHT], 512, 128)]
    to_left[...] = strip[at(sc[ROW_LEFT], 512, 128), 0:128]
    for block in range(7):
        kept[block * 64 : block * 64 + 64] = strip[at(2 * block + sc[YH], 64, 64)]


def widen_into(sc, lft, mid, rgt, out):
    @pl.when(sc[COL] == 0)
    def _():
        out[:, 0:256] = lft[...]
        out[:, 256:512] = mid[...]

    @pl.when(sc[COL] != 0)
    def _():
        out[:, 0:128] = lft[:, 128:256]
        out[:, 128:384] = mid[...]
        out[:, 384:512] = rgt[...]


def first_widen_kernel(sc, lft, mid, rgt, out):
    widen_into(sc, lft, mid, rgt, out)


def forward_tail(sc, w, p, tabs, far, keep, send, mid):
    meh, mel, moh, mol, teh, tel, toh, tol = tabs
    wr, wi = w[0], w[1]
    pr, pi = p[0], p[1]
    er = pr * wr - pi * wi
    ei = pr * wi + pi * wr
    total = jnp.concatenate([er[:HALF] + er[HALF:], ei[:HALF] + ei[HALF:]], axis=0)
    mid[0] = left(meh, mel, total)
    total = jnp.concatenate([er[:HALF] - er[HALF:], ei[:HALF] - ei[HALF:]], axis=0)
    mid[1] = left(moh, mol, total)
    core = sc[CORE]
    power = (jnp.sum(pr * pr) + jnp.sum(pi * pi)) * (1.0 / (PR * PR))
    for parity in (0, 1):
        rows = slice(parity * HALF, parity * HALF + HALF)
        yr, yi = mid[parity, 0:HALF], mid[parity, HALF:PR]
        total = jnp.concatenate([yr[:, :HALF] + yr[:, HALF:], yi[:, :HALF] + yi[:, HALF:]], axis=1)
        even = right(total, teh, tel)
        total = jnp.concatenate([yr[:, :HALF] - yr[:, HALF:], yi[:, :HALF] - yi[:, HALF:]], axis=1)
        odd = right(total, toh, tol)
        fr = jnp.concatenate([even[:, :HALF], odd[:, :HALF]], axis=1)
        fi = jnp.concatenate([even[:, HALF:], odd[:, HALF:]], axis=1)
        far[0, rows] = fr
        far[1, rows] = fi
        own = fr * fr + fi * fi

        @pl.when(core == parity)
        def _():
            keep[0:HALF] = own

        @pl.when(core != parity)
        def _():
            send[0:HALF] = own

    keep[HALF : HALF + 8] = jnp.full((8, PR), power, F32)
    send[HALF : HALF + 8] = jnp.full((8, PR), power, F32)


def forward_first_kernel(sc, mine, other, p, *rest):
    tabs, (w, far, keep, send, mid) = rest[:8], rest[8:]
    core = sc[CORE]
    w[core] = mine[...]
    w[1 - core] = other[...]
    forward_tail(sc, w, p, tabs, far, keep, send, mid)


def forward_second_kernel(sc, *rest):
    pieces, parts, tabs, (w, p, far, keep, send, mid) = rest[:4], rest[4:12], rest[12:20], rest[20:]
    core, yh, x, z = sc[CORE], sc[YH], sc[X], sc[Z]
    for which, piece in enumerate(pieces):
        plane = core if which < 2 else 1 - core
        parity = yh if which % 2 == 0 else 1 - yh
        for block in range(4):
            w[plane, at(2 * block + parity, 64, 64)] = piece[block * 64 : block * 64 + 64]
    for d in range(4):
        p[0, at(lax.rem(x + 4 - d, 4), 128, 128)] = parts[d][...]
        p[1, at(lax.rem(z + 4 - d, 4), 128, 128)] = parts[4 + d][...]
    forward_tail(sc, w, p, tabs, far, keep, send, mid)


FLOPS = 3 * 8 * PR**3
FIELD = (2, PR, PR)
EXT = (HALF + 8, PR)


def forward_first(sc, mine, other, p, tabs):
    return call(
        forward_first_kernel,
        sc,
        (mine, other, p, *tabs),
        (FIELD, FIELD, EXT, EXT),
        scratch=(FIELD,),
        limit=24,
        flops=FLOPS,
    )


def forward_second(sc, pieces, parts, tabs):
    return call(
        forward_second_kernel,
        sc,
        (*pieces, *parts, *tabs),
        (FIELD, FIELD, FIELD, EXT, EXT),
        scratch=(FIELD,),
        limit=24,
        flops=FLOPS,
    )


def inverse_kernel(sc, p, far, mine, other, *rest):
    tabs, (keep, send, chi, mid, weight) = rest[:8], rest[8:]
    meh, mel, moh, mol, teh, tel, toh, tol = tabs
    core = sc[CORE]
    weight[core] = mine[...]
    weight[1 - core] = other[...]
    for parity in (0, 1):
        rows = slice(parity * HALF, parity * HALF + HALF)
        yr = far[0, rows] * weight[parity]
        yi = far[1, rows] * weight[parity]
        even = right(jnp.concatenate([yr[:, :HALF], yi[:, :HALF]], axis=1), meh, mel)
        odd = right(jnp.concatenate([yr[:, HALF:], yi[:, HALF:]], axis=1), moh, mol)
        total = even + odd
        diff = even - odd
        mid[parity, 0:HALF] = jnp.concatenate([total[:, :HALF], diff[:, :HALF]], axis=1)
        mid[parity, HALF:PR] = jnp.concatenate([total[:, HALF:], diff[:, HALF:]], axis=1)
    even = left(teh, tel, mid[0])
    odd = left(toh, tol, mid[1])
    for top in (0, 1):
        rows = slice(top * HALF, top * HALF + HALF)
        both = even - odd if top else even + odd
        cr, ci = both[:HALF], both[HALF:]
        chi[0, rows] = cr
        chi[1, rows] = ci
        pr, pi = p[0, rows], p[1, rows]
        gr = pr * cr + pi * ci
        gi = pr * ci - pi * cr

        @pl.when(core == 0)
        def _():
            keep[rows] = gr
            send[rows] = gi

        @pl.when(core != 0)
        def _():
            keep[rows] = gi
            send[rows] = gr


def inverse(sc, p, far, mine, other, tabs):
    return call(
        inverse_kernel,
        sc,
        (p, far, mine, other, *tabs),
        ((PR, PR), (PR, PR), FIELD),
        scratch=(FIELD, (2, HALF, PR)),
        limit=24,
        flops=FLOPS,
    )


def probe_gradient_kernel(sc, w, chi, grad, power):
    wr, wi = w[0], w[1]
    cr, ci = chi[0], chi[1]
    grad[0] = wr * cr + wi * ci
    grad[1] = wr * ci - wi * cr
    total = (jnp.sum(wr * wr) + jnp.sum(wi * wi)) * (1.0 / (PR * PR))
    power[...] = jnp.full((8, PR), total, F32)


def stage_one_kernel(sc, keep, got, grad, power, stay, go, a0, a1, a2, a3, b0, b1, b2, b3):
    yh, x, z = sc[YH], sc[X], sc[Z]
    for block in range(4):
        rows = slice(block * 64, block * 64 + 64)
        here = at(2 * block + yh, 64, 64)
        there = at(2 * block + 1 - yh, 64, 64)
        stay[rows] = keep[here] + got[here]
        go[rows] = keep[there] + got[there]
    for d, (a, b) in enumerate(((a0, b0), (a1, b1), (a2, b2), (a3, b3))):
        a[0:128] = grad[0, at(lax.rem(x + d, 4), 128, 128)]
        a[128:136] = power[...]
        b[...] = grad[1, at(lax.rem(z + d, 4), 128, 128)]


def stage_two_kernel(sc, stay, got, a0, a1, a2, a3, b0, b1, b2, b3, *rest):
    (lft, mid, rgt), out_a, out_b, (sum_a, sum_b) = rest[:3], rest[3:7], rest[7:11], rest[11:]
    g = stay[...] + got[...]

    @pl.when(sc[COL] == 0)
    def _():
        lft[...] = g[:, 0:256]
        mid[...] = g[:, 256:512]
        rgt[...] = jnp.zeros(rgt.shape, F32)

    @pl.when(sc[COL] != 0)
    def _():
        lft[:, 0:128] = jnp.zeros((g.shape[0], 128), F32)
        lft[:, 128:256] = g[:, 0:128]
        mid[...] = g[:, 128:384]
        rgt[...] = g[:, 384:512]

    sum_a[...] = (a0[...] + a1[...]) + (a2[...] + a3[...])
    sum_b[...] = (b0[...] + b1[...]) + (b2[...] + b3[...])
    for d in range(4):
        out_a[d][0:32] = sum_a[at(lax.rem(sc[Z] + d, 4), 32, 32)]
        out_a[d][32:40] = sum_a[128:136]
        out_b[d][...] = sum_b[at(lax.rem(sc[X] + d, 4), 32, 32)]


def stage_three_kernel(
    sc, mid, from_right, from_left, a0, a1, a2, a3, b0, b1, b2, b3, strip, to_up, to_down, total
):
    strip[...] = jnp.zeros(strip.shape, F32)
    strip[at(sc[ROW], 256, 64)] = mid[...]
    rows = at(sc[ROW_RIGHT], 256, 64)
    strip[rows] = strip[rows] + from_right[...]
    rows = at(sc[ROW_LEFT], 256, 64)
    strip[rows, 0:128] = strip[rows, 0:128] + from_left[...]
    to_up[...] = strip[0:192]
    to_down[...] = strip[256:448]
    total[0:32] = (a0[0:32] + a1[0:32]) + (a2[0:32] + a3[0:32])
    total[32:64] = (b0[...] + b1[...]) + (b2[...] + b3[...])
    total[64:72] = (a0[32:40] + a1[32:40]) + (a2[32:40] + a3[32:40])


def probe_rows(sc, p, total, got, out_a, out_b):
    x, z = sc[X], sc[Z]
    both = total[...] + got[...]
    scale = 1.0 / both[64:65, 0:1]
    out_a[...] = p[0, at(4 * x + z, 32, 32)] - both[0:32] * scale
    out_b[...] = p[1, at(4 * z + x, 32, 32)] - both[32:64] * scale


def stage_four_kernel(
    sc, old, strip, from_up, from_down, power, p, total, got,
    mid, to_right, to_left, new, out_a, out_b,
):
    z = sc[Z]
    scale = 1.0 / (2.0 * power[0:1, 0:1])
    above = jnp.where(z == 0, 0.0, 1.0)
    below = jnp.where(z == 3, 0.0, 1.0)
    new[0:128] = (old[0:128] - (strip[0:128] + from_up[0:128]) * scale) * above
    new[128:192] = old[128:192] - (strip[128:192] + from_up[128:192]) * scale
    new[192:256] = old[192:256] - strip[192:256] * scale
    new[256:384] = old[256:384] - (strip[256:384] + from_down[0:128]) * scale
    new[384:448] = (old[384:448] - (strip[384:448] + from_down[128:192]) * scale) * below
    mid[...] = new[at(sc[ROW], 256, 64)]
    to_right[...] = new[at(sc[ROW_RIGHT], 256, 64)]
    to_left[...] = new[at(sc[ROW_LEFT], 256, 64), 0:128]
    probe_rows(sc, p, total, got, out_a, out_b)


def last_four_kernel(sc, old, strip, from_up, from_down, power, p, total, got, new, out_a, out_b):
    scale = 1.0 / (2.0 * power[0:1, 0:1])
    new[0:64] = old[128:192] - (strip[128:192] + from_up[128:192]) * scale
    new[64:128] = old[192:256] - strip[192:256] * scale
    new[128:256] = old[256:384] - (strip[256:384] + from_down[0:128]) * scale
    probe_rows(sc, p, total, got, out_a, out_b)


def gather_rows(sc, a0, a1, a2, a3, b0, b1, b2, b3, out_a, out_b):
    for d, (a, b) in enumerate(((a0, b0), (a1, b1), (a2, b2), (a3, b3))):
        out_a[at(lax.rem(sc[Z] + 4 - d, 4), 32, 32)] = a[...]
        out_b[at(lax.rem(sc[X] + 4 - d, 4), 32, 32)] = b[...]


def stage_five_kernel(sc, lft, mid, rgt, a0, a1, a2, a3, b0, b1, b2, b3, out, out_a, out_b):
    widen_into(sc, lft, mid, rgt, out)
    gather_rows(sc, a0, a1, a2, a3, b0, b1, b2, b3, out_a, out_b)


def last_five_kernel(sc, a0, a1, a2, a3, b0, b1, b2, b3, out_a, out_b):
    gather_rows(sc, a0, a1, a2, a3, b0, b1, b2, b3, out_a, out_b)


def join_field_kernel(sc, aa, ab, ba, bb, out):
    core, yh = sc[CORE], sc[YH]
    for block in range(4):
        rows = slice(block * 64, block * 64 + 64)
        out[core, at(2 * block + yh, 64, 64)] = aa[rows]
        out[core, at(2 * block + 1 - yh, 64, 64)] = ab[rows]
        out[1 - core, at(2 * block + yh, 64, 64)] = ba[rows]
        out[1 - core, at(2 * block + 1 - yh, 64, 64)] = bb[rows]


def join_probe_kernel(sc, a0, a1, a2, a3, b0, b1, b2, b3, out):
    for d, (a, b) in enumerate(((a0, b0), (a1, b1), (a2, b2), (a3, b3))):
        out[0, at(lax.rem(sc[X] + 4 - d, 4), 128, 128)] = a[...]
        out[1, at(lax.rem(sc[Z] + 4 - d, 4), 128, 128)] = b[...]


def swap_core(v):
    return lax.ppermute(v, "mode", [(0, 1), (1, 0), (2, 3), (3, 2)])


def swap_plane(v):
    return lax.ppermute(v, "mode", [(0, 2), (2, 0), (1, 3), (3, 1)])


def swap_y(v):
    return lax.ppermute(v, "tx", [(i, (i + 4) % 8) for i in range(8)])


def ring_x(v, d):
    return lax.ppermute(v, "tx", [(4 * y + i, 4 * y + (i + d) % 4) for y in range(2) for i in range(4)])


def ring_z(v, d):
    return lax.ppermute(v, "ty", [(i, (i + d) % 4) for i in range(4)])


def step(v, axis, d):
    count = {"ty": 4, "tx": 8}[axis]
    return lax.ppermute(v, axis, [(i, i + d) for i in range(count) if 0 <= i + d < count])


def around(first, second, parts_a, parts_b):
    got_a = [parts_a[0]] + [first(parts_a[d], d) for d in (1, 2, 3)]
    got_b = [parts_b[0]] + [second(parts_b[d], d) for d in (1, 2, 3)]
    return (*got_a, *got_b)


def gradients(sc, w, p, chi, keep, send, power, old, last):
    got = swap_core(send)
    grad, window_power = call(probe_gradient_kernel, sc, (w, chi), (FIELD, (8, PR)), limit=16)
    outs = call(
        stage_one_kernel,
        sc,
        (keep, got, grad, window_power),
        ((HALF, PR), (HALF, PR)) + ((136, PR),) * 4 + ((128, PR),) * 4,
        limit=12,
    )
    stay, go = outs[:2]
    got = swap_plane(go)
    parts = around(ring_x, ring_z, outs[2:6], outs[6:10])
    outs = call(
        stage_two_kernel,
        sc,
        (stay, got, *parts),
        ((HALF, 256), (HALF, 256), (HALF, 128)) + ((40, PR),) * 4 + ((32, PR),) * 4,
        scratch=((136, PR), (128, PR)),
        limit=8,
    )
    lft, mid, rgt = outs[:3]
    from_right, from_left = step(lft, "tx", -1), step(rgt, "tx", 1)
    parts = around(ring_z, ring_x, outs[3:7], outs[7:11])
    strip, to_up, to_down, total = call(
        stage_three_kernel,
        sc,
        (mid, from_right, from_left, *parts),
        ((448, 256), (192, 256), (192, 256), (72, PR)),
    )
    from_up, from_down, got = step(to_down, "ty", 1), step(to_up, "ty", -1), swap_y(total)
    ins = (old, strip, from_up, from_down, power, p, total, got)
    if last:
        new, a, b = call(last_four_kernel, sc, ins, ((256, 256), (32, PR), (32, PR)), limit=8)
        window = (new,)
        parts = around(ring_z, ring_x, (a,) * 4, (b,) * 4)
        a, b = call(last_five_kernel, sc, parts, ((128, PR), (128, PR)))
    else:
        mid, to_right, to_left, new, a, b = call(
            stage_four_kernel,
            sc,
            ins,
            ((256, 256), (256, 256), (256, 128), (448, 256), (32, PR), (32, PR)),
            limit=8,
        )
        lft, rgt = step(to_right, "tx", 1), step(to_left, "tx", -1)
        parts = around(ring_z, ring_x, (a,) * 4, (b,) * 4)
        window, a, b = call(
            stage_five_kernel,
            sc,
            (lft, mid, rgt, *parts),
            ((256, PR), (128, PR), (128, PR)),
        )
        window = (window,)
    aa = window[0]
    ab = swap_plane(aa)
    pieces = (aa, ab, swap_core(aa), swap_core(ab))
    return pieces, around(ring_x, ring_z, (a,) * 4, (b,) * 4), new


def weights(amp, keep, send):
    half = keep + swap_core(send)
    total = half + swap_plane(half)
    mine = 1.0 - amp / jnp.maximum(jnp.sqrt(total[:HALF]), 1.0)
    return mine, swap_core(mine), total[HALF:]


def body(object_field, probe, amplitudes, positions, owned):
    ty, tx, mode = lax.axis_index("ty"), lax.axis_index("tx"), lax.axis_index("mode")
    tile = ty * 8 + tx
    tiles = positions[:, 0] // 512 * 8 + positions[:, 1] // 256
    row_blocks = positions[:, 0] % 512 // 128
    col_blocks = positions[:, 1] % 256 // 128

    def pick(values, which):
        return jnp.sum(jnp.where(tiles == which, values, 0))

    core = mode % 2
    sc = jnp.stack(
        [
            pick(row_blocks, tile),
            pick(col_blocks, tile),
            pick(row_blocks, tile - 1),
            pick(row_blocks, tile + 1),
            tx % 4,
            ty,
            tx // 4,
            mode // 2,
            core,
        ]
    ).astype(jnp.int32)
    tabs = [jnp.asarray(t) for t in tables()]
    p = probe[:, 0]
    amp = call(order_kernel, sc, (amplitudes[0],), ((HALF, PR),), limit=24)[0]

    plane = lax.dynamic_index_in_dim(object_field, core, 0, keepdims=False)
    up, down = step(plane[256:512], "ty", 1), step(plane[0:128], "ty", -1)
    mid, to_right, to_left, strip = call(
        first_strips_kernel,
        sc,
        (up, plane, down),
        ((512, 256), (512, 256), (512, 128), (448, 256)),
        scratch=((896, 256),),
        limit=8,
    )
    lft, rgt = step(to_right, "tx", 1), step(to_left, "tx", -1)
    mine = call(first_widen_kernel, sc, (lft, mid, rgt), ((PR, PR),))[0]

    w, far, keep, send = forward_first(sc, mine, swap_core(mine), p, tabs)
    weight, weight_other, power = weights(amp, keep, send)
    keep, send, chi = inverse(sc, p, far, weight, weight_other, tabs)
    pieces, parts, strip = gradients(sc, w, p, chi, keep, send, power, strip, False)

    w, p, far, keep, send = forward_second(sc, pieces, parts, tabs)
    weight, weight_other, power = weights(amp, keep, send)
    keep, send, chi = inverse(sc, p, far, weight, weight_other, tabs)
    pieces, parts, _ = gradients(sc, w, p, chi, keep, send, power, strip, True)
    out_field = call(join_field_kernel, sc, pieces, ((2, 512, 256),))[0]
    out_probe = call(join_probe_kernel, sc, parts, (FIELD,), limit=8)[0]
    return out_field, out_probe[:, None]


def solution(mesh):
    placed = (
        P(None, "ty", "tx"),
        P(None, "mode", None, None),
        P(("ty", "tx"), None, None),
        P(),
        P(("ty", "tx"), None),
    )
    return jax.shard_map(
        body,
        mesh=mesh,
        in_specs=placed,
        out_specs=(P(None, "ty", "tx"), P(None, "mode", None, None)),
        check_vma=False,
    )
```

```python
import functools

import jax
import jax.numpy as jnp
import numpy as np
from jax import lax
from jax.experimental import pallas as pl
from jax.experimental.pallas import tpu as pltpu
from jax.sharding import PartitionSpec as P

PR = 512
HALF = 256
F32 = jnp.float32
BF16 = jnp.bfloat16
MIB = 1 << 20

ROW, COL, ROW_LEFT, ROW_RIGHT, X, Z, YL, YH, CORE = range(9)


def split_np(matrix):
    high = matrix.astype(jnp.bfloat16)
    low = (matrix - high.astype(np.float64)).astype(jnp.bfloat16)
    return high, low


def tables():
    k = np.arange(HALF)[:, None]
    u = np.arange(HALF)[None, :]
    out = []
    for odd in (0, 1):
        angle = 2.0 * np.pi * (((2 * k + odd) * u) % PR) / PR
        c, s = np.cos(angle) / np.sqrt(PR), np.sin(angle) / np.sqrt(PR)
        out.append(np.block([[c, s], [-s, c]]))
    even, odd = out
    parts = []
    for m in (even, odd, even.T, odd.T):
        parts.extend(split_np(np.ascontiguousarray(m)))
    return parts


def split(x):
    high = x.astype(BF16)
    return high, (x - high.astype(F32)).astype(BF16)


def dot(a, b):
    return jnp.dot(a, b, preferred_element_type=F32)


def left(mh, ml, x):
    xh, xl = split(x)
    return dot(mh[...], xh) + (dot(mh[...], xl) + dot(ml[...], xh))


def right(x, mh, ml):
    xh, xl = split(x)
    return dot(xh, mh[...]) + (dot(xl, mh[...]) + dot(xh, ml[...]))


def smem():
    return pl.BlockSpec(memory_space=pltpu.SMEM)


def vmem():
    return pl.BlockSpec(memory_space=pltpu.VMEM)


def call(kernel, sc, ins, outs, scratch=(), limit=6, flops=0):
    return pl.pallas_call(
        kernel,
        out_shape=[jax.ShapeDtypeStruct(s, F32) for s in outs],
        in_specs=[smem()] + [vmem()] * len(ins),
        out_specs=[vmem()] * len(outs),
        scratch_shapes=[pltpu.VMEM(s, F32) for s in scratch],
        compiler_params=pltpu.CompilerParams(vmem_limit_bytes=limit * MIB),
        cost_estimate=pl.CostEstimate(
            flops=flops,
            bytes_accessed=4 * sum(int(np.prod(s)) for s in outs) + sum(a.nbytes for a in ins),
            transcendentals=0,
        ),
    )(sc, *ins)


def at(start, size, unit):
    return pl.ds(pl.multiple_of(start * unit, unit), size)


def exact_parts(x):
    a = x.astype(BF16)
    rest = x - a.astype(F32)
    b = rest.astype(BF16)
    return a, b, (rest - b.astype(F32)).astype(BF16)


def order_kernel(sc, amp, out):
    core = sc[CORE]
    row = lax.broadcasted_iota(jnp.int32, (HALF, PR), 0)
    col = lax.broadcasted_iota(jnp.int32, (HALF, PR), 1)
    pick = jnp.where(col == 2 * row + core, 1.0, 0.0).astype(BF16)
    a, b, c = exact_parts(amp[...])
    rows = (dot(pick, a) + dot(pick, b)) + dot(pick, c)
    src = lax.broadcasted_iota(jnp.int32, (PR, PR), 0)
    dst = lax.broadcasted_iota(jnp.int32, (PR, PR), 1)
    want = jnp.where(dst < HALF, 2 * dst, 2 * (dst - HALF) + 1)
    move = jnp.where(src == want, 1.0, 0.0).astype(BF16)
    a, b, c = exact_parts(rows)
    out[...] = (dot(a, move) + dot(b, move)) + dot(c, move)


def first_strips_kernel(sc, up, own, down, mid, to_right, to_left, kept, strip):
    strip[0:256] = up[...]
    strip[256:768] = own[...]
    strip[768:896] = down[...]
    mid[...] = strip[at(sc[ROW], 512, 128)]
    to_right[...] = strip[at(sc[ROW_RIGHT], 512, 128)]
    to_left[...] = strip[at(sc[ROW_LEFT], 512, 128), 0:128]
    for block in range(7):
        kept[block * 64 : block * 64 + 64] = strip[at(2 * block + sc[YH], 64, 64)]


def widen_into(sc, lft, mid, rgt, out):
    @pl.when(sc[COL] == 0)
    def _():
        out[:, 0:256] = lft[...]
        out[:, 256:512] = mid[...]

    @pl.when(sc[COL] != 0)
    def _():
        out[:, 0:128] = lft[:, 128:256]
        out[:, 128:384] = mid[...]
        out[:, 384:512] = rgt[...]


def first_widen_kernel(sc, lft, mid, rgt, out):
    widen_into(sc, lft, mid, rgt, out)


def forward_tail(sc, w, p, tabs, far, keep, send, mid):
    meh, mel, moh, mol, teh, tel, toh, tol = tabs
    wr, wi = w[0], w[1]
    pr, pi = p[0], p[1]
    er = pr * wr - pi * wi
    ei = pr * wi + pi * wr
    total = jnp.concatenate([er[:HALF] + er[HALF:], ei[:HALF] + ei[HALF:]], axis=0)
    mid[0] = left(meh, mel, total)
    total = jnp.concatenate([er[:HALF] - er[HALF:], ei[:HALF] - ei[HALF:]], axis=0)
    mid[1] = left(moh, mol, total)
    core = sc[CORE]
    power = (jnp.sum(pr * pr) + jnp.sum(pi * pi)) * (1.0 / (PR * PR))
    for parity in (0, 1):
        rows = slice(parity * HALF, parity * HALF + HALF)
        yr, yi = mid[parity, 0:HALF], mid[parity, HALF:PR]
        total = jnp.concatenate([yr[:, :HALF] + yr[:, HALF:], yi[:, :HALF] + yi[:, HALF:]], axis=1)
        even = right(total, teh, tel)
        total = jnp.concatenate([yr[:, :HALF] - yr[:, HALF:], yi[:, :HALF] - yi[:, HALF:]], axis=1)
        odd = right(total, toh, tol)
        fr = jnp.concatenate([even[:, :HALF], odd[:, :HALF]], axis=1)
        fi = jnp.concatenate([even[:, HALF:], odd[:, HALF:]], axis=1)
        far[0, rows] = fr
        far[1, rows] = fi
        own = fr * fr + fi * fi

        @pl.when(core == parity)
        def _():
            keep[0:HALF] = own

        @pl.when(core != parity)
        def _():
            send[0:HALF] = own

    keep[HALF : HALF + 8] = jnp.full((8, PR), power, F32)
    send[HALF : HALF + 8] = jnp.full((8, PR), power, F32)


def forward_first_kernel(sc, mine, other, p, *rest):
    tabs, (w, far, keep, send, mid) = rest[:8], rest[8:]
    core = sc[CORE]
    w[core] = mine[...]
    w[1 - core] = other[...]
    forward_tail(sc, w, p, tabs, far, keep, send, mid)


def forward_second_kernel(sc, aa, ab, ba, bb, old, mine, got, *rest):
    tabs, (w, p, far, keep, send, mid) = rest[:8], rest[8:]
    core, yh = sc[CORE], sc[YH]
    for plane, parity, piece in (
        (core, yh, aa),
        (core, 1 - yh, ab),
        (1 - core, yh, ba),
        (1 - core, 1 - yh, bb),
    ):
        for block in range(4):
            w[plane, at(2 * block + parity, 64, 64)] = piece[block * 64 : block * 64 + 64]
    p[core] = old[core] - mine[...]
    p[1 - core] = old[1 - core] - got[...]
    forward_tail(sc, w, p, tabs, far, keep, send, mid)


FLOPS = 3 * 8 * PR**3
FIELD = (2, PR, PR)
EXT = (HALF + 8, PR)


def forward_first(sc, mine, other, p, tabs):
    return call(
        forward_first_kernel,
        sc,
        (mine, other, p, *tabs),
        (FIELD, FIELD, EXT, EXT),
        scratch=(FIELD,),
        limit=24,
        flops=FLOPS,
    )


def forward_second(sc, pieces, p, parts, tabs):
    return call(
        forward_second_kernel,
        sc,
        (*pieces, p, *parts, *tabs),
        (FIELD, FIELD, FIELD, EXT, EXT),
        scratch=(FIELD,),
        limit=24,
        flops=FLOPS,
    )


def inverse_kernel(sc, p, far, mine, other, *rest):
    tabs, (keep, send, chi, mid, weight) = rest[:8], rest[8:]
    meh, mel, moh, mol, teh, tel, toh, tol = tabs
    core = sc[CORE]
    weight[core] = mine[...]
    weight[1 - core] = other[...]
    for parity in (0, 1):
        rows = slice(parity * HALF, parity * HALF + HALF)
        yr = far[0, rows] * weight[parity]
        yi = far[1, rows] * weight[parity]
        even = right(jnp.concatenate([yr[:, :HALF], yi[:, :HALF]], axis=1), meh, mel)
        odd = right(jnp.concatenate([yr[:, HALF:], yi[:, HALF:]], axis=1), moh, mol)
        total = even + odd
        diff = even - odd
        mid[parity, 0:HALF] = jnp.concatenate([total[:, :HALF], diff[:, :HALF]], axis=1)
        mid[parity, HALF:PR] = jnp.concatenate([total[:, HALF:], diff[:, HALF:]], axis=1)
    even = left(teh, tel, mid[0])
    odd = left(toh, tol, mid[1])
    for top in (0, 1):
        rows = slice(top * HALF, top * HALF + HALF)
        both = even - odd if top else even + odd
        cr, ci = both[:HALF], both[HALF:]
        chi[0, rows] = cr
        chi[1, rows] = ci
        pr, pi = p[0, rows], p[1, rows]
        gr = pr * cr + pi * ci
        gi = pr * ci - pi * cr

        @pl.when(core == 0)
        def _():
            keep[rows] = gr
            send[rows] = gi

        @pl.when(core != 0)
        def _():
            keep[rows] = gi
            send[rows] = gr


def inverse(sc, p, far, mine, other, tabs):
    return call(
        inverse_kernel,
        sc,
        (p, far, mine, other, *tabs),
        ((PR, PR), (PR, PR), FIELD),
        scratch=(FIELD, (2, HALF, PR)),
        limit=24,
        flops=FLOPS,
    )


def probe_gradient_kernel(sc, w, chi, mine, theirs, power):
    wr, wi = w[0], w[1]
    cr, ci = chi[0], chi[1]
    gr = wr * cr + wi * ci
    gi = wr * ci - wi * cr

    @pl.when(sc[CORE] == 0)
    def _():
        mine[...] = gr
        theirs[...] = gi

    @pl.when(sc[CORE] != 0)
    def _():
        mine[...] = gi
        theirs[...] = gr

    total = (jnp.sum(wr * wr) + jnp.sum(wi * wi)) * (1.0 / (PR * PR))
    power[...] = jnp.full((8, PR), total, F32)


def halve_kernel(sc, keep, got, stay, go):
    yh = sc[YH]
    for block in range(4):
        rows = slice(block * 64, block * 64 + 64)
        here = at(2 * block + yh, 64, 64)
        there = at(2 * block + 1 - yh, 64, 64)
        stay[rows] = keep[here] + got[here]
        go[rows] = keep[there] + got[there]


def ring_place(sc):
    return jnp.where(sc[CORE] == 0, sc[X], sc[Z])


def chunk_kernel(sc, mine, got, power, *outs):
    place, core = ring_place(sc), sc[CORE]
    for d, out in enumerate(outs):
        rows = at(lax.rem(place + d, 4), 128, 128)
        out[at(core, 128, 128)] = mine[rows]
        out[at(1 - core, 128, 128)] = got[rows]
        out[256:264] = power[...]


def stage_two_kernel(sc, stay, got, c0, c1, c2, c3, lft, mid, rgt, total):
    g = stay[...] + got[...]

    @pl.when(sc[COL] == 0)
    def _():
        lft[...] = g[:, 0:256]
        mid[...] = g[:, 256:512]
        rgt[...] = jnp.zeros(rgt.shape, F32)

    @pl.when(sc[COL] != 0)
    def _():
        lft[:, 0:128] = jnp.zeros((g.shape[0], 128), F32)
        lft[:, 128:256] = g[:, 0:128]
        mid[...] = g[:, 128:384]
        rgt[...] = g[:, 384:512]

    total[...] = (c0[...] + c1[...]) + (c2[...] + c3[...])


def stage_three_kernel(sc, mid, from_right, from_left, part, got, strip, to_up, to_down, total):
    strip[...] = jnp.zeros(strip.shape, F32)
    strip[at(sc[ROW], 256, 64)] = mid[...]
    rows = at(sc[ROW_RIGHT], 256, 64)
    strip[rows] = strip[rows] + from_right[...]
    rows = at(sc[ROW_LEFT], 256, 64)
    strip[rows, 0:128] = strip[rows, 0:128] + from_left[...]
    to_up[...] = strip[0:192]
    to_down[...] = strip[256:448]
    total[...] = part[...] + got[...]


def stage_four_kernel(
    sc, old, strip, from_up, from_down, power, part, got,
    mid, to_right, to_left, new, total,
):
    z = sc[Z]
    scale = 1.0 / (2.0 * power[0:1, 0:1])
    above = jnp.where(z == 0, 0.0, 1.0)
    below = jnp.where(z == 3, 0.0, 1.0)
    new[0:128] = (old[0:128] - (strip[0:128] + from_up[0:128]) * scale) * above
    new[128:192] = old[128:192] - (strip[128:192] + from_up[128:192]) * scale
    new[192:256] = old[192:256] - strip[192:256] * scale
    new[256:384] = old[256:384] - (strip[256:384] + from_down[0:128]) * scale
    new[384:448] = (old[384:448] - (strip[384:448] + from_down[128:192]) * scale) * below
    mid[...] = new[at(sc[ROW], 256, 64)]
    to_right[...] = new[at(sc[ROW_RIGHT], 256, 64)]
    to_left[...] = new[at(sc[ROW_LEFT], 256, 64), 0:128]
    total[...] = part[...] + got[...]


def last_four_kernel(sc, old, strip, from_up, from_down, power, part, got, new, total):
    scale = 1.0 / (2.0 * power[0:1, 0:1])
    new[0:64] = old[128:192] - (strip[128:192] + from_up[128:192]) * scale
    new[64:128] = old[192:256] - strip[192:256] * scale
    new[128:256] = old[256:384] - (strip[256:384] + from_down[0:128]) * scale
    total[...] = part[...] + got[...]


def finish_sum(part, got, total):
    scale = 1.0 / (part[256:257, 0:1] + got[256:257, 0:1])
    total[...] = (part[0:256] + got[0:256]) * scale


def stage_five_kernel(sc, lft, mid, rgt, part, got, out, total):
    widen_into(sc, lft, mid, rgt, out)
    finish_sum(part, got, total)


def last_five_kernel(sc, part, got, total):
    finish_sum(part, got, total)


def collect_kernel(sc, c0, c1, c2, c3, mine, theirs):
    place, core = ring_place(sc), sc[CORE]
    for d, part in enumerate((c0, c1, c2, c3)):
        rows = at(lax.rem(place + 4 - d, 4), 128, 128)
        mine[rows] = part[at(core, 128, 128)]
        theirs[rows] = part[at(1 - core, 128, 128)]


def join_probe_kernel(sc, old, mine, got, out):
    core = sc[CORE]
    out[core] = old[core] - mine[...]
    out[1 - core] = old[1 - core] - got[...]


def join_field_kernel(sc, aa, ab, ba, bb, out):
    core, yh = sc[CORE], sc[YH]
    for block in range(4):
        rows = slice(block * 64, block * 64 + 64)
        out[core, at(2 * block + yh, 64, 64)] = aa[rows]
        out[core, at(2 * block + 1 - yh, 64, 64)] = ab[rows]
        out[1 - core, at(2 * block + yh, 64, 64)] = ba[rows]
        out[1 - core, at(2 * block + 1 - yh, 64, 64)] = bb[rows]


def swap_core(v):
    return lax.ppermute(v, "mode", [(0, 1), (1, 0), (2, 3), (3, 2)])


def swap_plane(v):
    return lax.ppermute(v, "mode", [(0, 2), (2, 0), (1, 3), (3, 1)])


def permute(v, move):
    pairs = []
    for z in range(4):
        for y in range(2):
            for x in range(4):
                for mode in range(4):
                    tx, ty, tz = move(mode % 2, x, y, z)
                    pairs.append((((z * 2 + y) * 4 + x) * 4 + mode, ((tz * 2 + ty) * 4 + tx) * 4 + mode))
    return lax.ppermute(v, ("ty", "tx", "mode"), pairs)


def ring(v, d):
    return permute(v, lambda core, x, y, z: (x, y, (z + d) % 4) if core else ((x + d) % 4, y, z))


def pair_one(v):
    return permute(v, lambda core, x, y, z: (x, 1 - y, z) if core else (x, y, z ^ 1))


def pair_two(v):
    return permute(v, lambda core, x, y, z: (x ^ 1, y, z) if core else (x, 1 - y, z))


def pair_three(v):
    return permute(v, lambda core, x, y, z: (3 - x, y, z) if core else (x, y, 3 - z))


def step(v, axis, d):
    count = {"ty": 4, "tx": 8}[axis]
    return lax.ppermute(v, axis, [(i, i + d) for i in range(count) if 0 <= i + d < count])


def gradients(sc, w, p, chi, keep, send, power, old, last):
    got = swap_core(send)
    mine, theirs, window_power = call(
        probe_gradient_kernel, sc, (w, chi), ((PR, PR), (PR, PR), (8, PR)), limit=16
    )
    other = swap_core(theirs)
    stay, go = call(halve_kernel, sc, (keep, got), ((HALF, PR), (HALF, PR)), limit=8)
    got = swap_plane(go)
    chunks = call(chunk_kernel, sc, (mine, other, window_power), ((264, PR),) * 4, limit=8)
    chunks = [chunks[0]] + [ring(chunks[d], d) for d in (1, 2, 3)]
    lft, mid, rgt, part = call(
        stage_two_kernel,
        sc,
        (stay, got, *chunks),
        ((HALF, 256), (HALF, 256), (HALF, 128), (264, PR)),
        limit=8,
    )
    from_right, from_left, got = step(lft, "tx", -1), step(rgt, "tx", 1), pair_one(part)
    strip, to_up, to_down, part = call(
        stage_three_kernel,
        sc,
        (mid, from_right, from_left, part, got),
        ((448, 256), (192, 256), (192, 256), (264, PR)),
    )
    from_up, from_down, got = step(to_down, "ty", 1), step(to_up, "ty", -1), pair_two(part)
    ins = (old, strip, from_up, from_down, power, part, got)
    if last:
        new, part = call(last_four_kernel, sc, ins, ((256, 256), (264, PR)))
        aa = new
        total = call(last_five_kernel, sc, (part, pair_three(part)), ((256, PR),))[0]
    else:
        mid, to_right, to_left, new, part = call(
            stage_four_kernel,
            sc,
            ins,
            ((256, 256), (256, 256), (256, 128), (448, 256), (264, PR)),
        )
        lft, rgt = step(to_right, "tx", 1), step(to_left, "tx", -1)
        aa, total = call(
            stage_five_kernel,
            sc,
            (lft, mid, rgt, part, pair_three(part)),
            ((256, PR), (256, PR)),
        )
    ab = swap_plane(aa)
    pieces = (aa, ab, swap_core(aa), swap_core(ab))
    chunks = (total, ring(total, 1), ring(total, 2), ring(total, 3))
    mine, theirs = call(collect_kernel, sc, chunks, ((PR, PR), (PR, PR)), limit=8)
    return pieces, (mine, swap_core(theirs)), new


def weights(amp, keep, send):
    half = keep + swap_core(send)
    total = half + swap_plane(half)
    mine = 1.0 - amp / jnp.maximum(jnp.sqrt(total[:HALF]), 1.0)
    return mine, swap_core(mine), total[HALF:]


def body(object_field, probe, amplitudes, positions, owned):
    ty, tx, mode = lax.axis_index("ty"), lax.axis_index("tx"), lax.axis_index("mode")
    tile = ty * 8 + tx
    tiles = positions[:, 0] // 512 * 8 + positions[:, 1] // 256
    row_blocks = positions[:, 0] % 512 // 128
    col_blocks = positions[:, 1] % 256 // 128

    def pick(values, which):
        return jnp.sum(jnp.where(tiles == which, values, 0))

    core = mode % 2
    sc = jnp.stack(
        [
            pick(row_blocks, tile),
            pick(col_blocks, tile),
            pick(row_blocks, tile - 1),
            pick(row_blocks, tile + 1),
            tx % 4,
            ty,
            tx // 4,
            mode // 2,
            core,
        ]
    ).astype(jnp.int32)
    tabs = [jnp.asarray(t) for t in tables()]
    p = probe[:, 0]
    amp = call(order_kernel, sc, (amplitudes[0],), ((HALF, PR),), limit=24)[0]

    plane = lax.dynamic_index_in_dim(object_field, core, 0, keepdims=False)
    up, down = step(plane[256:512], "ty", 1), step(plane[0:128], "ty", -1)
    mid, to_right, to_left, strip = call(
        first_strips_kernel,
        sc,
        (up, plane, down),
        ((512, 256), (512, 256), (512, 128), (448, 256)),
        scratch=((896, 256),),
        limit=8,
    )
    lft, rgt = step(to_right, "tx", 1), step(to_left, "tx", -1)
    mine = call(first_widen_kernel, sc, (lft, mid, rgt), ((PR, PR),))[0]

    w, far, keep, send = forward_first(sc, mine, swap_core(mine), p, tabs)
    weight, weight_other, power = weights(amp, keep, send)
    keep, send, chi = inverse(sc, p, far, weight, weight_other, tabs)
    pieces, parts, strip = gradients(sc, w, p, chi, keep, send, power, strip, False)

    w, p, far, keep, send = forward_second(sc, pieces, p, parts, tabs)
    weight, weight_other, power = weights(amp, keep, send)
    keep, send, chi = inverse(sc, p, far, weight, weight_other, tabs)
    pieces, parts, _ = gradients(sc, w, p, chi, keep, send, power, strip, True)
    out_field = call(join_field_kernel, sc, pieces, ((2, 512, 256),))[0]
    out_probe = call(join_probe_kernel, sc, (p, *parts), (FIELD,), limit=12)[0]
    return out_field, out_probe[:, None]


def solution(mesh):
    placed = (
        P(None, "ty", "tx"),
        P(None, "mode", None, None),
        P(("ty", "tx"), None, None),
        P(),
        P(("ty", "tx"), None),
    )
    return jax.shard_map(
        body,
        mesh=mesh,
        in_specs=placed,
        out_specs=(P(None, "ty", "tx"), P(None, "mode", None, None)),
        check_vma=False,
    )
```

```python
import functools

import jax
import jax.numpy as jnp
import numpy as np
from jax import lax
from jax.experimental import pallas as pl
from jax.experimental.pallas import tpu as pltpu
from jax.sharding import PartitionSpec as P

PR = 512
HALF = 256
F32 = jnp.float32
BF16 = jnp.bfloat16
MIB = 1 << 20

ROW, COL, ROW_LEFT, ROW_RIGHT, X, Z, YL, YH, CORE = range(9)


def split_np(matrix):
    high = matrix.astype(jnp.bfloat16)
    low = (matrix - high.astype(np.float64)).astype(jnp.bfloat16)
    return high, low


def tables():
    k = np.arange(HALF)[:, None]
    u = np.arange(HALF)[None, :]
    out = []
    for odd in (0, 1):
        angle = 2.0 * np.pi * (((2 * k + odd) * u) % PR) / PR
        c, s = np.cos(angle) / np.sqrt(PR), np.sin(angle) / np.sqrt(PR)
        out.append(np.block([[c, s], [-s, c]]))
    even, odd = out
    parts = []
    for m in (even, odd, even.T, odd.T):
        parts.extend(split_np(np.ascontiguousarray(m)))
    return parts


def split(x):
    high = x.astype(BF16)
    return high, (x - high.astype(F32)).astype(BF16)


def dot(a, b):
    return jnp.dot(a, b, preferred_element_type=F32)


def left(mh, ml, x):
    xh, xl = split(x)
    return dot(mh[...], xh) + (dot(mh[...], xl) + dot(ml[...], xh))


def right(x, mh, ml):
    xh, xl = split(x)
    return dot(xh, mh[...]) + (dot(xl, mh[...]) + dot(xh, ml[...]))


def right_t(x, mh, ml):
    def dot_t(a, b):
        return lax.dot_general(a, b, (((1,), (1,)), ((), ())), preferred_element_type=F32)

    xh, xl = split(x)
    return dot_t(xh, mh[...]) + (dot_t(xl, mh[...]) + dot_t(xh, ml[...]))


def smem():
    return pl.BlockSpec(memory_space=pltpu.SMEM)


def vmem():
    return pl.BlockSpec(memory_space=pltpu.VMEM)


def even_row(sc):
    return lax.rem(sc[Z], 2) == 0


def row_sides(sc, got_first, got_second):
    even = even_row(sc)
    return jnp.where(even, got_second, got_first), jnp.where(even, got_first, got_second)


def row_sends(sc, to_up, to_down, first, second):
    @pl.when(even_row(sc))
    def _():
        first[...] = to_down
        second[...] = to_up

    @pl.when(jnp.logical_not(even_row(sc)))
    def _():
        first[...] = to_up
        second[...] = to_down


def call(kernel, sc, ins, outs, scratch=(), limit=6, flops=0, after=()):
    count = len(ins)

    def run(sc_ref, *refs):
        kernel(sc_ref, *refs[:count], *refs[count + len(after) :])

    return pl.pallas_call(
        run,
        out_shape=[jax.ShapeDtypeStruct(s, F32) for s in outs],
        in_specs=[smem()] + [vmem()] * count + [pl.BlockSpec(memory_space=pl.ANY)] * len(after),
        out_specs=[vmem()] * len(outs),
        scratch_shapes=[pltpu.VMEM(s, F32) for s in scratch],
        compiler_params=pltpu.CompilerParams(vmem_limit_bytes=limit * MIB),
        cost_estimate=pl.CostEstimate(
            flops=flops,
            bytes_accessed=4 * sum(int(np.prod(s)) for s in outs) + sum(a.nbytes for a in ins),
            transcendentals=0,
        ),
    )(sc, *ins, *after)


def at(start, size, unit):
    return pl.ds(pl.multiple_of(start * unit, unit), size)


def exact_parts(x):
    a = x.astype(BF16)
    rest = x - a.astype(F32)
    b = rest.astype(BF16)
    return a, b, (rest - b.astype(F32)).astype(BF16)


def order_kernel(sc, amp, out):
    core = sc[CORE]
    row = lax.broadcasted_iota(jnp.int32, (HALF, PR), 0)
    col = lax.broadcasted_iota(jnp.int32, (HALF, PR), 1)
    pick = jnp.where(col == 2 * row + core, 1.0, 0.0).astype(BF16)
    a, b, c = exact_parts(amp[...])
    rows = (dot(pick, a) + dot(pick, b)) + dot(pick, c)
    src = lax.broadcasted_iota(jnp.int32, (PR, PR), 0)
    dst = lax.broadcasted_iota(jnp.int32, (PR, PR), 1)
    want = jnp.where(dst < HALF, 2 * dst, 2 * (dst - HALF) + 1)
    move = jnp.where(src == want, 1.0, 0.0).astype(BF16)
    a, b, c = exact_parts(rows)
    out[...] = (dot(a, move) + dot(b, move)) + dot(c, move)


def first_strips_kernel(sc, up, own, down, mid, to_right, to_left, kept, strip):
    strip[0:256] = up[...]
    strip[256:768] = own[...]
    strip[768:896] = down[...]
    mid[...] = strip[at(sc[ROW], 512, 128)]
    to_right[...] = strip[at(sc[ROW_RIGHT], 512, 128)]
    to_left[...] = strip[at(sc[ROW_LEFT], 512, 128), 0:128]
    for block in range(7):
        kept[block * 64 : block * 64 + 64] = strip[at(2 * block + sc[YH], 64, 64)]


def widen_kernel(sc, lft, mid, rgt, out):
    column = 4 * sc[YL] + sc[X]

    @pl.when(sc[COL] == 0)
    def _():
        out[:, 0:256] = jnp.where(column == 0, 0.0, lft[...])
        out[:, 256:512] = mid[...]

    @pl.when(sc[COL] != 0)
    def _():
        out[:, 0:128] = jnp.where(column == 0, 0.0, lft[:, 128:256])
        out[:, 128:384] = mid[...]
        out[:, 384:512] = jnp.where(column == 7, 0.0, rgt[...])


def forward_tail(sc, w, p, tabs, far, keep, send, mid):
    meh, mel, moh, mol = tabs
    wr, wi = w[0], w[1]
    pr, pi = p[0], p[1]
    er = pr * wr - pi * wi
    ei = pr * wi + pi * wr
    total = jnp.concatenate([er[:HALF] + er[HALF:], ei[:HALF] + ei[HALF:]], axis=0)
    mid[0] = left(meh, mel, total)
    total = jnp.concatenate([er[:HALF] - er[HALF:], ei[:HALF] - ei[HALF:]], axis=0)
    mid[1] = left(moh, mol, total)
    core = sc[CORE]
    power = (jnp.sum(pr * pr) + jnp.sum(pi * pi)) * (1.0 / (PR * PR))
    for parity in (0, 1):
        rows = slice(parity * HALF, parity * HALF + HALF)
        yr, yi = mid[parity, 0:HALF], mid[parity, HALF:PR]
        total = jnp.concatenate([yr[:, :HALF] + yr[:, HALF:], yi[:, :HALF] + yi[:, HALF:]], axis=1)
        even = right_t(total, meh, mel)
        total = jnp.concatenate([yr[:, :HALF] - yr[:, HALF:], yi[:, :HALF] - yi[:, HALF:]], axis=1)
        odd = right_t(total, moh, mol)
        fr = jnp.concatenate([even[:, :HALF], odd[:, :HALF]], axis=1)
        fi = jnp.concatenate([even[:, HALF:], odd[:, HALF:]], axis=1)
        far[0, rows] = fr
        far[1, rows] = fi
        own = fr * fr + fi * fi

        @pl.when(core == parity)
        def _():
            keep[0:HALF] = own

        @pl.when(core != parity)
        def _():
            send[0:HALF] = own

    keep[HALF : HALF + 8] = jnp.full((8, PR), power, F32)
    send[HALF : HALF + 8] = jnp.full((8, PR), power, F32)


def forward_first_kernel(sc, mine, other, p, *rest):
    tabs, (w, far, keep, send, mid) = rest[:4], rest[4:]
    core = sc[CORE]
    w[core] = mine[...]
    w[1 - core] = other[...]
    forward_tail(sc, w, p, tabs, far, keep, send, mid)


def forward_second_kernel(sc, aa, ab, ba, bb, old, mine, got, *rest):
    tabs, (w, p, far, keep, send, mid) = rest[:4], rest[4:]
    core, yh = sc[CORE], sc[YH]
    for plane, parity, piece in (
        (core, yh, aa),
        (core, 1 - yh, ab),
        (1 - core, yh, ba),
        (1 - core, 1 - yh, bb),
    ):
        for block in range(4):
            w[plane, at(2 * block + parity, 64, 64)] = piece[block * 64 : block * 64 + 64]
    p[core] = old[core] - mine[...]
    p[1 - core] = old[1 - core] - got[...]
    forward_tail(sc, w, p, tabs, far, keep, send, mid)


FLOPS = 3 * 8 * PR**3
FIELD = (2, PR, PR)
EXT = (HALF + 8, PR)


def forward_first(sc, mine, other, p, tabs):
    return call(
        forward_first_kernel,
        sc,
        (mine, other, p, *tabs[:4]),
        (FIELD, FIELD, EXT, EXT),
        scratch=(FIELD,),
        limit=24,
        flops=FLOPS,
    )


def forward_second(sc, pieces, p, parts, tabs):
    return call(
        forward_second_kernel,
        sc,
        (*pieces, p, *parts, *tabs[:4]),
        (FIELD, FIELD, FIELD, EXT, EXT),
        scratch=(FIELD,),
        limit=24,
        flops=FLOPS,
    )


def inverse_kernel(sc, w, p, far, mine, other, *rest):
    tabs, (keep, send, stay, go, power, mid, weight) = rest[:8], rest[8:]
    meh, mel, moh, mol, teh, tel, toh, tol = tabs
    core = sc[CORE]
    weight[core] = mine[...]
    weight[1 - core] = other[...]
    for parity in (0, 1):
        rows = slice(parity * HALF, parity * HALF + HALF)
        yr = far[0, rows] * weight[parity]
        yi = far[1, rows] * weight[parity]
        even = right(jnp.concatenate([yr[:, :HALF], yi[:, :HALF]], axis=1), meh, mel)
        odd = right(jnp.concatenate([yr[:, HALF:], yi[:, HALF:]], axis=1), moh, mol)
        total = even + odd
        diff = even - odd
        mid[parity, 0:HALF] = jnp.concatenate([total[:, :HALF], diff[:, :HALF]], axis=1)
        mid[parity, HALF:PR] = jnp.concatenate([total[:, HALF:], diff[:, HALF:]], axis=1)
    even = left(teh, tel, mid[0])
    odd = left(toh, tol, mid[1])
    squares = jnp.zeros((), F32)
    for top in (0, 1):
        rows = slice(top * HALF, top * HALF + HALF)
        both = even - odd if top else even + odd
        cr, ci = both[:HALF], both[HALF:]
        pr, pi = p[0, rows], p[1, rows]
        wr, wi = w[0, rows], w[1, rows]
        for vr, vi, own, swap in ((pr, pi, keep, send), (wr, wi, stay, go)):
            gr = vr * cr + vi * ci
            gi = vr * ci - vi * cr

            @pl.when(core == 0)
            def _():
                own[rows] = gr
                swap[rows] = gi

            @pl.when(core != 0)
            def _():
                own[rows] = gi
                swap[rows] = gr

        squares = squares + (jnp.sum(wr * wr) + jnp.sum(wi * wi))
    power[...] = jnp.full((8, PR), squares * (1.0 / (PR * PR)), F32)


def inverse(sc, w, p, far, mine, other, tabs):
    return call(
        inverse_kernel,
        sc,
        (w, p, far, mine, other, *tabs),
        ((PR, PR), (PR, PR), (PR, PR), (PR, PR), (8, PR)),
        scratch=(FIELD, (2, HALF, PR)),
        limit=24,
        flops=FLOPS,
    )


def halve_kernel(sc, keep, got, stay, go):
    yh = sc[YH]
    for block in range(4):
        rows = slice(block * 64, block * 64 + 64)
        here = at(2 * block + yh, 64, 64)
        there = at(2 * block + 1 - yh, 64, 64)
        stay[rows] = keep[here] + got[here]
        go[rows] = keep[there] + got[there]


def ring_place(sc):
    return jnp.where(sc[CORE] == 0, sc[X], sc[Z])


def chunk_kernel(sc, mine, got, power, *outs):
    place, core = ring_place(sc), sc[CORE]
    for d, out in enumerate(outs):
        rows = at(lax.rem(place + d, 4), 128, 128)
        out[at(core, 128, 128)] = mine[rows]
        out[at(1 - core, 128, 128)] = got[rows]
        out[256:264] = power[...]


def fold_kernel(sc, stay, got, lft, mid, rgt):
    g = stay[...] + got[...]

    @pl.when(sc[COL] == 0)
    def _():
        lft[...] = g[:, 0:256]
        mid[...] = g[:, 256:512]
        rgt[...] = jnp.zeros(rgt.shape, F32)

    @pl.when(sc[COL] != 0)
    def _():
        lft[:, 0:128] = jnp.zeros((g.shape[0], 128), F32)
        lft[:, 128:256] = g[:, 0:128]
        mid[...] = g[:, 128:384]
        rgt[...] = g[:, 384:512]


def ring_sum_kernel(sc, c0, c1, c2, c3, total):
    total[...] = (c0[...] + c1[...]) + (c2[...] + c3[...])


def stage_three_kernel(sc, mid, from_right, from_left, part, got, strip, first, second, total):
    column = 4 * sc[YL] + sc[X]
    strip[...] = jnp.zeros(strip.shape, F32)
    strip[at(sc[ROW], 256, 64)] = mid[...]
    rows = at(sc[ROW_RIGHT], 256, 64)
    strip[rows] = strip[rows] + jnp.where(column == 7, 0.0, from_right[...])
    rows = at(sc[ROW_LEFT], 256, 64)
    strip[rows, 0:128] = strip[rows, 0:128] + jnp.where(column == 0, 0.0, from_left[...])
    row_sends(sc, strip[0:192], strip[256:448], first, second)
    total[...] = part[...] + got[...]


def stage_four_kernel(
    sc, old, strip, got_first, got_second, power, part, got,
    mid, to_right, to_left, new, total,
):
    z = sc[Z]
    from_up, from_down = row_sides(sc, got_first[...], got_second[...])
    scale = 1.0 / (2.0 * power[0:1, 0:1])
    above = jnp.where(z == 0, 0.0, 1.0)
    below = jnp.where(z == 3, 0.0, 1.0)
    new[0:128] = (old[0:128] - (strip[0:128] + from_up[0:128]) * scale) * above
    new[128:192] = old[128:192] - (strip[128:192] + from_up[128:192]) * scale
    new[192:256] = old[192:256] - strip[192:256] * scale
    new[256:384] = old[256:384] - (strip[256:384] + from_down[0:128]) * scale
    new[384:448] = (old[384:448] - (strip[384:448] + from_down[128:192]) * scale) * below
    mid[...] = new[at(sc[ROW], 256, 64)]
    to_right[...] = new[at(sc[ROW_RIGHT], 256, 64)]
    to_left[...] = new[at(sc[ROW_LEFT], 256, 64), 0:128]
    total[...] = part[...] + got[...]


def last_four_kernel(sc, old, strip, got_first, got_second, power, part, got, new, total):
    from_up, from_down = row_sides(sc, got_first[...], got_second[...])
    scale = 1.0 / (2.0 * power[0:1, 0:1])
    new[0:64] = old[128:192] - (strip[128:192] + from_up[128:192]) * scale
    new[64:128] = old[192:256] - strip[192:256] * scale
    new[128:256] = old[256:384] - (strip[256:384] + from_down[0:128]) * scale
    total[...] = part[...] + got[...]


def finish_sum_kernel(sc, part, got, total):
    scale = 1.0 / (part[256:257, 0:1] + got[256:257, 0:1])
    total[...] = (part[0:256] + got[0:256]) * scale


def collect_kernel(sc, c0, c1, c2, c3, mine, theirs):
    place, core = ring_place(sc), sc[CORE]
    for d, part in enumerate((c0, c1, c2, c3)):
        rows = at(lax.rem(place + 4 - d, 4), 128, 128)
        mine[rows] = part[at(core, 128, 128)]
        theirs[rows] = part[at(1 - core, 128, 128)]


def join_probe_kernel(sc, old, mine, got, out):
    core = sc[CORE]
    out[core] = old[core] - mine[...]
    out[1 - core] = old[1 - core] - got[...]


def join_field_kernel(sc, aa, ab, ba, bb, out):
    core, yh = sc[CORE], sc[YH]
    for block in range(4):
        rows = slice(block * 64, block * 64 + 64)
        out[core, at(2 * block + yh, 64, 64)] = aa[rows]
        out[core, at(2 * block + 1 - yh, 64, 64)] = ab[rows]
        out[1 - core, at(2 * block + yh, 64, 64)] = ba[rows]
        out[1 - core, at(2 * block + 1 - yh, 64, 64)] = bb[rows]


def swap_core(v):
    return lax.ppermute(v, "mode", [(0, 1), (1, 0), (2, 3), (3, 2)])


def swap_plane(v):
    return lax.ppermute(v, "mode", [(0, 2), (2, 0), (1, 3), (3, 1)])


def permute(v, move):
    pairs = []
    for z in range(4):
        for y in range(2):
            for x in range(4):
                for mode in range(4):
                    tx, ty, tz = move(mode % 2, x, y, z)
                    pairs.append((((z * 2 + y) * 4 + x) * 4 + mode, ((tz * 2 + ty) * 4 + tx) * 4 + mode))
    return lax.ppermute(v, ("ty", "tx", "mode"), pairs)


def ring(v, d):
    return permute(v, lambda core, x, y, z: (x, y, (z + d) % 4) if core else ((x + d) % 4, y, z))


def pair_one(v):
    return permute(v, lambda core, x, y, z: (x, 1 - y, z) if core else (x, y, z ^ 1))


def pair_two(v):
    return permute(v, lambda core, x, y, z: (x ^ 1, y, z) if core else (x, 1 - y, z))


def pair_three(v):
    return permute(v, lambda core, x, y, z: (3 - x, y, z) if core else (x, y, 3 - z))


def step(v, axis, d):
    count = {"ty": 4, "tx": 8}[axis]
    return lax.ppermute(v, axis, [(i, i + d) for i in range(count) if 0 <= i + d < count])


def shift(v, d):
    return lax.ppermute(v, "tx", [(i, (i + d) % 8) for i in range(8)])


def swap_rows(first, second):
    return (
        lax.ppermute(first, "ty", [(0, 1), (1, 0), (2, 3), (3, 2)]),
        lax.ppermute(second, "ty", [(1, 2), (2, 1)]),
    )


def fold_gradients(sc, w, p, far, weight, weight_other, tabs):
    keep, send, mine, theirs, window_power = inverse(sc, w, p, far, weight, weight_other, tabs)
    got = swap_core(send)
    other = swap_core(theirs)
    stay, go = call(halve_kernel, sc, (keep, got), ((HALF, PR), (HALF, PR)), limit=8)
    got = swap_plane(go)
    chunks = call(
        chunk_kernel, sc, (mine, other, window_power), ((264, PR),) * 4, limit=8, after=(go,)
    )
    chunks = [chunks[0]] + [ring(chunks[d], d) for d in (1, 2, 3)]
    lft, mid, rgt = call(
        fold_kernel, sc, (stay, got), ((HALF, 256), (HALF, 256), (HALF, 128)), limit=8, flops=6 * 10**9
    )
    part = call(ring_sum_kernel, sc, chunks, ((264, PR),), after=(lft,))[0]
    from_right, from_left, got = shift(lft, -1), shift(rgt, 1), pair_one(part)
    strip, first, second, part = call(
        stage_three_kernel,
        sc,
        (mid, from_right, from_left, part, got),
        ((448, 256), (192, 256), (192, 256), (264, PR)),
    )
    first, second = swap_rows(first, second)
    return strip, first, second, part, pair_two(part)


def spread(total):
    return total, ring(total, 1), ring(total, 2), ring(total, 3)


def update(sc, old, folded, power):
    strip, first, second, part, got = folded
    mid, to_right, to_left, new, part = call(
        stage_four_kernel,
        sc,
        (old, strip, first, second, power, part, got),
        ((256, 256), (256, 256), (256, 128), (448, 256), (264, PR)),
    )
    lft, rgt, got = shift(to_right, 1), shift(to_left, -1), pair_three(part)
    aa = call(widen_kernel, sc, (lft, mid, rgt), ((256, PR),))[0]
    ab = swap_plane(aa)
    total = call(finish_sum_kernel, sc, (part, got), ((256, PR),), after=(aa,))[0]
    pieces = (aa, ab, swap_core(aa), swap_core(ab))
    mine, theirs = call(
        collect_kernel, sc, spread(total), ((PR, PR), (PR, PR)), limit=8, after=pieces[3:]
    )
    return pieces, (mine, swap_core(theirs)), new


def last_update(sc, p, old, folded, power):
    strip, first, second, part, got = folded
    aa, part = call(
        last_four_kernel,
        sc,
        (old, strip, first, second, power, part, got),
        ((256, 256), (264, PR)),
    )
    got = pair_three(part)
    ab = swap_plane(aa)
    total = call(finish_sum_kernel, sc, (part, got), ((256, PR),), after=(ab,))[0]
    pieces = (aa, ab, swap_core(aa), swap_core(ab))
    field = call(join_field_kernel, sc, pieces, ((2, 512, 256),))[0]
    mine, theirs = call(
        collect_kernel, sc, spread(total), ((PR, PR), (PR, PR)), limit=8, after=(field,)
    )
    return field, call(join_probe_kernel, sc, (p, mine, swap_core(theirs)), (FIELD,), limit=12)[0]


def weights(amp, keep, send):
    half = keep + swap_core(send)
    total = half + swap_plane(half)
    mine = 1.0 - amp / jnp.maximum(jnp.sqrt(total[:HALF]), 1.0)
    return mine, swap_core(mine), total[HALF:]


def body(object_field, probe, amplitudes, positions, owned):
    ty, tx, mode = lax.axis_index("ty"), lax.axis_index("tx"), lax.axis_index("mode")
    tile = ty * 8 + tx
    tiles = positions[:, 0] // 512 * 8 + positions[:, 1] // 256
    row_blocks = positions[:, 0] % 512 // 128
    col_blocks = positions[:, 1] % 256 // 128

    def pick(values, which):
        return jnp.sum(jnp.where(tiles == which, values, 0))

    core = mode % 2
    sc = jnp.stack(
        [
            pick(row_blocks, tile),
            pick(col_blocks, tile),
            pick(row_blocks, tile - 1),
            pick(row_blocks, tile + 1),
            tx % 4,
            ty,
            tx // 4,
            mode // 2,
            core,
        ]
    ).astype(jnp.int32)
    tabs = [jnp.asarray(t) for t in tables()]
    p = probe[:, 0]
    amp = call(order_kernel, sc, (amplitudes[0],), ((HALF, PR),), limit=24)[0]

    plane = lax.dynamic_index_in_dim(object_field, core, 0, keepdims=False)
    up, down = step(plane[256:512], "ty", 1), step(plane[0:128], "ty", -1)
    mid, to_right, to_left, strip = call(
        first_strips_kernel,
        sc,
        (up, plane, down),
        ((512, 256), (512, 256), (512, 128), (448, 256)),
        scratch=((896, 256),),
        limit=8,
    )
    lft, rgt = step(to_right, "tx", 1), step(to_left, "tx", -1)
    mine = call(widen_kernel, sc, (lft, mid, rgt), ((PR, PR),))[0]

    w, far, keep, send = forward_first(sc, mine, swap_core(mine), p, tabs)
    weight, weight_other, power = weights(amp, keep, send)
    folded = fold_gradients(sc, w, p, far, weight, weight_other, tabs)
    pieces, parts, strip = update(sc, strip, folded, power)

    w, p, far, keep, send = forward_second(sc, pieces, p, parts, tabs)
    weight, weight_other, power = weights(amp, keep, send)
    folded = fold_gradients(sc, w, p, far, weight, weight_other, tabs)
    out_field, out_probe = last_update(sc, p, strip, folded, power)
    return out_field, out_probe[:, None]


def solution(mesh):
    placed = (
        P(None, "ty", "tx"),
        P(None, "mode", None, None),
        P(("ty", "tx"), None, None),
        P(),
        P(("ty", "tx"), None),
    )
    return jax.shard_map(
        body,
        mesh=mesh,
        in_specs=placed,
        out_specs=(P(None, "ty", "tx"), P(None, "mode", None, None)),
        check_vma=False,
    )
```

```python
import functools

import jax
import jax.numpy as jnp
import numpy as np
from jax import lax
from jax.experimental import pallas as pl
from jax.experimental.pallas import tpu as pltpu
from jax.sharding import PartitionSpec as P

PR = 512
HALF = 256
F32 = jnp.float32
BF16 = jnp.bfloat16
MIB = 1 << 20

ROW, COL, ROW_LEFT, ROW_RIGHT, X, Z, YL, YH, CORE = range(9)


def split_np(matrix):
    high = matrix.astype(jnp.bfloat16)
    low = (matrix - high.astype(np.float64)).astype(jnp.bfloat16)
    return high, low


def tables():
    k = np.arange(HALF)[:, None]
    u = np.arange(HALF)[None, :]
    out = []
    for odd in (0, 1):
        angle = 2.0 * np.pi * (((2 * k + odd) * u) % PR) / PR
        c, s = np.cos(angle) / np.sqrt(PR), np.sin(angle) / np.sqrt(PR)
        out.append(np.block([[c, s], [-s, c]]))
    even, odd = out
    parts = []
    for m in (even, odd, even.T, odd.T):
        parts.extend(split_np(np.ascontiguousarray(m)))
    return parts


def split(x):
    high = x.astype(BF16)
    return high, (x - high.astype(F32)).astype(BF16)


def dot(a, b):
    return jnp.dot(a, b, preferred_element_type=F32)


def left(mh, ml, x):
    xh, xl = split(x)
    return dot(mh[...], xh) + (dot(mh[...], xl) + dot(ml[...], xh))


def right(x, mh, ml):
    xh, xl = split(x)
    return dot(xh, mh[...]) + (dot(xl, mh[...]) + dot(xh, ml[...]))


def right_t(x, mh, ml):
    def dot_t(a, b):
        return lax.dot_general(a, b, (((1,), (1,)), ((), ())), preferred_element_type=F32)

    xh, xl = split(x)
    return dot_t(xh, mh[...]) + (dot_t(xl, mh[...]) + dot_t(xh, ml[...]))


def smem():
    return pl.BlockSpec(memory_space=pltpu.SMEM)


def vmem():
    return pl.BlockSpec(memory_space=pltpu.VMEM)


def even_row(sc):
    return lax.rem(sc[Z], 2) == 0


def row_sides(sc, got_first, got_second):
    even = even_row(sc)
    return jnp.where(even, got_second, got_first), jnp.where(even, got_first, got_second)


def row_sends(sc, to_up, to_down, first, second):
    @pl.when(even_row(sc))
    def _():
        first[...] = to_down
        second[...] = to_up

    @pl.when(jnp.logical_not(even_row(sc)))
    def _():
        first[...] = to_up
        second[...] = to_down


def call(kernel, sc, ins, outs, scratch=(), limit=6, flops=0, after=()):
    count = len(ins)

    def run(sc_ref, *refs):
        kernel(sc_ref, *refs[:count], *refs[count + len(after) :])

    return pl.pallas_call(
        run,
        out_shape=[jax.ShapeDtypeStruct(s, F32) for s in outs],
        in_specs=[smem()] + [vmem()] * count + [pl.BlockSpec(memory_space=pl.ANY)] * len(after),
        out_specs=[vmem()] * len(outs),
        scratch_shapes=[pltpu.VMEM(s, F32) for s in scratch],
        compiler_params=pltpu.CompilerParams(vmem_limit_bytes=limit * MIB),
        cost_estimate=pl.CostEstimate(
            flops=flops,
            bytes_accessed=4 * sum(int(np.prod(s)) for s in outs) + sum(a.nbytes for a in ins),
            transcendentals=0,
        ),
    )(sc, *ins, *after)


def at(start, size, unit):
    return pl.ds(pl.multiple_of(start * unit, unit), size)


def exact_parts(x):
    a = x.astype(BF16)
    rest = x - a.astype(F32)
    b = rest.astype(BF16)
    return a, b, (rest - b.astype(F32)).astype(BF16)


def order_kernel(sc, amp, out):
    core = sc[CORE]
    row = lax.broadcasted_iota(jnp.int32, (HALF, PR), 0)
    col = lax.broadcasted_iota(jnp.int32, (HALF, PR), 1)
    pick = jnp.where(col == 2 * row + core, 1.0, 0.0).astype(BF16)
    a, b, c = exact_parts(amp[...])
    rows = (dot(pick, a) + dot(pick, b)) + dot(pick, c)
    src = lax.broadcasted_iota(jnp.int32, (PR, PR), 0)
    dst = lax.broadcasted_iota(jnp.int32, (PR, PR), 1)
    want = jnp.where(dst < HALF, 2 * dst, 2 * (dst - HALF) + 1)
    move = jnp.where(src == want, 1.0, 0.0).astype(BF16)
    a, b, c = exact_parts(rows)
    out[...] = (dot(a, move) + dot(b, move)) + dot(c, move)


def first_strips_kernel(sc, up, own, down, mid, to_right, to_left, kept, strip):
    strip[0:256] = up[...]
    strip[256:768] = own[...]
    strip[768:896] = down[...]
    mid[...] = strip[at(sc[ROW], 512, 128)]
    to_right[...] = strip[at(sc[ROW_RIGHT], 512, 128)]
    to_left[...] = strip[at(sc[ROW_LEFT], 512, 128), 0:128]
    for block in range(7):
        kept[block * 64 : block * 64 + 64] = strip[at(2 * block + sc[YH], 64, 64)]


def widen_kernel(sc, lft, mid, rgt, out):
    column = 4 * sc[YL] + sc[X]

    @pl.when(sc[COL] == 0)
    def _():
        out[:, 0:256] = jnp.where(column == 0, 0.0, lft[...])
        out[:, 256:512] = mid[...]

    @pl.when(sc[COL] != 0)
    def _():
        out[:, 0:128] = jnp.where(column == 0, 0.0, lft[:, 128:256])
        out[:, 128:384] = mid[...]
        out[:, 384:512] = jnp.where(column == 7, 0.0, rgt[...])


def left_side(w, p, tabs, mid):
    meh, mel, moh, mol = tabs
    wr, wi = w[0], w[1]
    pr, pi = p[0], p[1]
    er = pr * wr - pi * wi
    ei = pr * wi + pi * wr
    total = jnp.concatenate([er[:HALF] + er[HALF:], ei[:HALF] + ei[HALF:]], axis=0)
    mid[0] = left(meh, mel, total)
    total = jnp.concatenate([er[:HALF] - er[HALF:], ei[:HALF] - ei[HALF:]], axis=0)
    mid[1] = left(moh, mol, total)
    return (jnp.sum(pr * pr) + jnp.sum(pi * pi)) * (1.0 / (PR * PR))


def right_side(mid, parity, tabs, far, intensity):
    meh, mel, moh, mol = tabs
    yr, yi = mid[parity, 0:HALF], mid[parity, HALF:PR]
    total = jnp.concatenate([yr[:, :HALF] + yr[:, HALF:], yi[:, :HALF] + yi[:, HALF:]], axis=1)
    even = right_t(total, meh, mel)
    total = jnp.concatenate([yr[:, :HALF] - yr[:, HALF:], yi[:, :HALF] - yi[:, HALF:]], axis=1)
    odd = right_t(total, moh, mol)
    fr = jnp.concatenate([even[:, :HALF], odd[:, :HALF]], axis=1)
    fi = jnp.concatenate([even[:, HALF:], odd[:, HALF:]], axis=1)
    far[0] = fr
    far[1] = fi
    intensity[0:HALF] = fr * fr + fi * fi


def forward_tail(sc, w, p, tabs, mid, far, send, power):
    mean = left_side(w, p, tabs, mid)
    right_side(mid, 1 - sc[CORE], tabs, far, send)
    send[HALF : HALF + 8] = jnp.full((8, PR), mean, F32)
    power[...] = jnp.full((8, PR), mean, F32)


def forward_rest_kernel(sc, mid, power, *rest):
    tabs, (far, keep) = rest[:4], rest[4:]
    right_side(mid, sc[CORE], tabs, far, keep)
    keep[HALF : HALF + 8] = power[...]


def forward_first_kernel(sc, mine, other, p, *rest):
    tabs, (w, mid, far, send, power) = rest[:4], rest[4:]
    core = sc[CORE]
    w[core] = mine[...]
    w[1 - core] = other[...]
    forward_tail(sc, w, p, tabs, mid, far, send, power)


def forward_second_kernel(sc, aa, ab, ba, bb, old, mine, got, *rest):
    tabs, (w, p, mid, far, send, power) = rest[:4], rest[4:]
    core, yh = sc[CORE], sc[YH]
    for plane, parity, piece in (
        (core, yh, aa),
        (core, 1 - yh, ab),
        (1 - core, yh, ba),
        (1 - core, 1 - yh, bb),
    ):
        for block in range(4):
            w[plane, at(2 * block + parity, 64, 64)] = piece[block * 64 : block * 64 + 64]
    p[core] = old[core] - mine[...]
    p[1 - core] = old[1 - core] - got[...]
    forward_tail(sc, w, p, tabs, mid, far, send, power)


FLOPS = 3 * 8 * PR**3
FIELD = (2, PR, PR)
EXT = (HALF + 8, PR)


FIRST = (FIELD, (2, HALF, PR), EXT, (8, PR))


def forward_first(sc, mine, other, p, tabs):
    outs = call(
        forward_first_kernel,
        sc,
        (mine, other, p, *tabs[:4]),
        (FIELD,) + FIRST,
        limit=24,
        flops=FLOPS * 3 // 4,
    )
    return outs[0], outs[1:]


def forward_second(sc, pieces, p, parts, tabs):
    outs = call(
        forward_second_kernel,
        sc,
        (*pieces, p, *parts, *tabs[:4]),
        (FIELD, FIELD) + FIRST,
        limit=24,
        flops=FLOPS * 3 // 4,
    )
    return outs[0], outs[1], outs[2:]


def measured_fields(sc, amp, first, tabs):
    mid, far_send, send, power = first
    got = swap_core(send)
    far_keep, keep = call(
        forward_rest_kernel,
        sc,
        (mid, power, *tabs[:4]),
        ((2, HALF, PR), EXT),
        limit=16,
        flops=FLOPS // 4,
    )
    half = keep + got
    total = half + swap_plane(half)
    mine = 1.0 - amp / jnp.maximum(jnp.sqrt(total[:HALF]), 1.0)
    other = swap_core(mine)
    back = call(
        inverse_rows_kernel,
        sc,
        (far_keep, mine, *tabs[:4]),
        ((PR, PR),),
        limit=16,
        flops=FLOPS // 4,
    )[0]
    return back, far_send, other, total[HALF:]


def inverse_rows(far, weight, tabs):
    meh, mel, moh, mol = tabs
    yr = far[0] * weight[...]
    yi = far[1] * weight[...]
    even = right(jnp.concatenate([yr[:, :HALF], yi[:, :HALF]], axis=1), meh, mel)
    odd = right(jnp.concatenate([yr[:, HALF:], yi[:, HALF:]], axis=1), moh, mol)
    total = even + odd
    diff = even - odd
    real = jnp.concatenate([total[:, :HALF], diff[:, :HALF]], axis=1)
    return real, jnp.concatenate([total[:, HALF:], diff[:, HALF:]], axis=1)


def inverse_rows_kernel(sc, far, weight, *rest):
    tabs, out = rest[:4], rest[4]
    out[0:HALF], out[HALF:PR] = inverse_rows(far, weight, tabs)


def inverse_kernel(sc, w, p, back, far, other, *rest):
    tabs, (keep, send, stay, go, power, mid) = rest[:8], rest[8:]
    teh, tel, toh, tol = tabs[4:]
    core = sc[CORE]
    mid[core] = back[...]
    mid[1 - core, 0:HALF], mid[1 - core, HALF:PR] = inverse_rows(far, other, tabs[:4])
    even = left(teh, tel, mid[0])
    odd = left(toh, tol, mid[1])
    squares = jnp.zeros((), F32)
    for top in (0, 1):
        rows = slice(top * HALF, top * HALF + HALF)
        both = even - odd if top else even + odd
        cr, ci = both[:HALF], both[HALF:]
        pr, pi = p[0, rows], p[1, rows]
        wr, wi = w[0, rows], w[1, rows]
        for vr, vi, own, swap in ((pr, pi, keep, send), (wr, wi, stay, go)):
            gr = vr * cr + vi * ci
            gi = vr * ci - vi * cr

            @pl.when(core == 0)
            def _():
                own[rows] = gr
                swap[rows] = gi

            @pl.when(core != 0)
            def _():
                own[rows] = gi
                swap[rows] = gr

        squares = squares + (jnp.sum(wr * wr) + jnp.sum(wi * wi))
    power[...] = jnp.full((8, PR), squares * (1.0 / (PR * PR)), F32)


def inverse(sc, w, p, back, far, other, tabs):
    return call(
        inverse_kernel,
        sc,
        (w, p, back, far, other, *tabs),
        ((PR, PR), (PR, PR), (PR, PR), (PR, PR), (8, PR)),
        scratch=(FIELD,),
        limit=24,
        flops=FLOPS * 3 // 4,
    )


def halve_kernel(sc, keep, got, stay, go):
    yh = sc[YH]
    for block in range(4):
        rows = slice(block * 64, block * 64 + 64)
        here = at(2 * block + yh, 64, 64)
        there = at(2 * block + 1 - yh, 64, 64)
        stay[rows] = keep[here] + got[here]
        go[rows] = keep[there] + got[there]


def ring_place(sc):
    return jnp.where(sc[CORE] == 0, sc[X], sc[Z])


def chunk_kernel(sc, mine, got, power, *outs):
    place, core = ring_place(sc), sc[CORE]
    for d, out in enumerate(outs):
        rows = at(lax.rem(place + d, 4), 128, 128)
        out[at(core, 128, 128)] = mine[rows]
        out[at(1 - core, 128, 128)] = got[rows]
        out[256:264] = power[...]


def fold_kernel(sc, stay, got, lft, mid, rgt):
    g = stay[...] + got[...]

    @pl.when(sc[COL] == 0)
    def _():
        lft[...] = g[:, 0:256]
        mid[...] = g[:, 256:512]
        rgt[...] = jnp.zeros(rgt.shape, F32)

    @pl.when(sc[COL] != 0)
    def _():
        lft[:, 0:128] = jnp.zeros((g.shape[0], 128), F32)
        lft[:, 128:256] = g[:, 0:128]
        mid[...] = g[:, 128:384]
        rgt[...] = g[:, 384:512]


def ring_sum_kernel(sc, c0, c1, c2, c3, total):
    total[...] = (c0[...] + c1[...]) + (c2[...] + c3[...])


def stage_three_kernel(sc, mid, from_right, from_left, part, got, strip, first, second, total):
    column = 4 * sc[YL] + sc[X]
    strip[...] = jnp.zeros(strip.shape, F32)
    strip[at(sc[ROW], 256, 64)] = mid[...]
    rows = at(sc[ROW_RIGHT], 256, 64)
    strip[rows] = strip[rows] + jnp.where(column == 7, 0.0, from_right[...])
    rows = at(sc[ROW_LEFT], 256, 64)
    strip[rows, 0:128] = strip[rows, 0:128] + jnp.where(column == 0, 0.0, from_left[...])
    row_sends(sc, strip[0:192], strip[256:448], first, second)
    total[...] = part[...] + got[...]


def stage_four_kernel(
    sc, old, strip, got_first, got_second, power, part, got,
    mid, to_right, to_left, new, total,
):
    z = sc[Z]
    from_up, from_down = row_sides(sc, got_first[...], got_second[...])
    scale = 1.0 / (2.0 * power[0:1, 0:1])
    above = jnp.where(z == 0, 0.0, 1.0)
    below = jnp.where(z == 3, 0.0, 1.0)
    new[0:128] = (old[0:128] - (strip[0:128] + from_up[0:128]) * scale) * above
    new[128:192] = old[128:192] - (strip[128:192] + from_up[128:192]) * scale
    new[192:256] = old[192:256] - strip[192:256] * scale
    new[256:384] = old[256:384] - (strip[256:384] + from_down[0:128]) * scale
    new[384:448] = (old[384:448] - (strip[384:448] + from_down[128:192]) * scale) * below
    mid[...] = new[at(sc[ROW], 256, 64)]
    to_right[...] = new[at(sc[ROW_RIGHT], 256, 64)]
    to_left[...] = new[at(sc[ROW_LEFT], 256, 64), 0:128]
    total[...] = part[...] + got[...]


def last_four_kernel(sc, old, strip, got_first, got_second, power, part, got, new, total):
    from_up, from_down = row_sides(sc, got_first[...], got_second[...])
    scale = 1.0 / (2.0 * power[0:1, 0:1])
    new[0:64] = old[128:192] - (strip[128:192] + from_up[128:192]) * scale
    new[64:128] = old[192:256] - strip[192:256] * scale
    new[128:256] = old[256:384] - (strip[256:384] + from_down[0:128]) * scale
    total[...] = part[...] + got[...]


def finish_sum_kernel(sc, part, got, total):
    scale = 1.0 / (part[256:257, 0:1] + got[256:257, 0:1])
    total[...] = (part[0:256] + got[0:256]) * scale


def last_sum_kernel(sc, part, got, old, mine, theirs):
    core = sc[CORE]
    scale = 1.0 / (part[256:257, 0:1] + got[256:257, 0:1])
    rows = at(core, 128, 128)
    here = at(ring_place(sc), 128, 128)
    mine[...] = old[core, here] - (part[rows] + got[rows]) * scale
    rows = at(1 - core, 128, 128)
    theirs[...] = (part[rows] + got[rows]) * scale


def other_place(sc):
    return jnp.where(sc[CORE] == 0, sc[Z], sc[X])


def last_step_kernel(sc, old, got, out):
    out[...] = old[1 - sc[CORE], at(other_place(sc), 128, 128)] - got[...]


def collect_kernel(sc, c0, c1, c2, c3, mine, theirs):
    place, core = ring_place(sc), sc[CORE]
    for d, part in enumerate((c0, c1, c2, c3)):
        rows = at(lax.rem(place + 4 - d, 4), 128, 128)
        mine[rows] = part[at(core, 128, 128)]
        theirs[rows] = part[at(1 - core, 128, 128)]


def join_probe_kernel(sc, *refs):
    parts, out = refs[:8], refs[8]
    core = sc[CORE]
    for n, part in enumerate(parts):
        plane, place = (core, ring_place(sc)) if n < 4 else (1 - core, other_place(sc))
        out[plane, at(lax.rem(place + 4 - n % 4, 4), 128, 128)] = part[...]


def join_field_kernel(sc, aa, ab, ba, bb, out, token):
    token[...] = jnp.zeros(token.shape, F32)
    core, yh = sc[CORE], sc[YH]
    for block in range(4):
        rows = slice(block * 64, block * 64 + 64)
        out[core, at(2 * block + yh, 64, 64)] = aa[rows]
        out[core, at(2 * block + 1 - yh, 64, 64)] = ab[rows]
        out[1 - core, at(2 * block + yh, 64, 64)] = ba[rows]
        out[1 - core, at(2 * block + 1 - yh, 64, 64)] = bb[rows]


def swap_core(v):
    return lax.ppermute(v, "mode", [(0, 1), (1, 0), (2, 3), (3, 2)])


def swap_plane(v):
    return lax.ppermute(v, "mode", [(0, 2), (2, 0), (1, 3), (3, 1)])


def permute(v, move):
    pairs = []
    for z in range(4):
        for y in range(2):
            for x in range(4):
                for mode in range(4):
                    tx, ty, tz = move(mode % 2, x, y, z)
                    pairs.append((((z * 2 + y) * 4 + x) * 4 + mode, ((tz * 2 + ty) * 4 + tx) * 4 + mode))
    return lax.ppermute(v, ("ty", "tx", "mode"), pairs)


def ring(v, d):
    return permute(v, lambda core, x, y, z: (x, y, (z + d) % 4) if core else ((x + d) % 4, y, z))


def other_ring(v, d):
    return permute(v, lambda core, x, y, z: ((x + d) % 4, y, z) if core else (x, y, (z + d) % 4))


def pair(v, turn, last):
    def move(core, x, y, z):
        if core == 0:
            return x, 1 - y if turn == 1 else y, (z ^ 1, z, 3 - z)[turn]
        x_turn = turn - 1 if last else turn
        if x_turn in (0, 1):
            return (x ^ 1, 3 - x)[x_turn], y, z
        return x, 1 - y, z

    return permute(v, move)


def step(v, axis, d):
    count = {"ty": 4, "tx": 8}[axis]
    return lax.ppermute(v, axis, [(i, i + d) for i in range(count) if 0 <= i + d < count])


def shift(v, d):
    return lax.ppermute(v, "tx", [(i, (i + d) % 8) for i in range(8)])


def swap_rows(first, second):
    return (
        lax.ppermute(first, "ty", [(0, 1), (1, 0), (2, 3), (3, 2)]),
        lax.ppermute(second, "ty", [(1, 2), (2, 1)]),
    )


EARLY = 6 * 10**9


def fold_gradients(sc, w, p, fields, tabs, last):
    keep, send, mine, theirs, window_power = inverse(sc, w, p, *fields, tabs)
    got = swap_core(send)
    other = swap_core(theirs)
    chunks = call(chunk_kernel, sc, (mine, other, window_power), ((264, PR),) * 4, limit=8)
    stay, go = call(
        halve_kernel, sc, (keep, got), ((HALF, PR), (HALF, PR)), limit=8, after=(chunks[0],)
    )
    got = swap_plane(go)
    chunks = [chunks[0]] + [ring(chunks[d], d) for d in (1, 2, 3)]
    part = call(ring_sum_kernel, sc, chunks, ((264, PR),), flops=EARLY)[0]
    lft, mid, rgt = call(
        fold_kernel, sc, (stay, got), ((HALF, 256), (HALF, 256), (HALF, 128)), limit=8, after=(part,)
    )
    from_right, from_left, got = shift(lft, -1), shift(rgt, 1), pair(part, 0, last)
    strip, first, second, part = call(
        stage_three_kernel,
        sc,
        (mid, from_right, from_left, part, got),
        ((448, 256), (192, 256), (192, 256), (264, PR)),
    )
    first, second = swap_rows(first, second)
    return strip, first, second, part, pair(part, 1, last)


def spread(total):
    return total, ring(total, 1), ring(total, 2), ring(total, 3)


def update(sc, old, folded, power):
    strip, first, second, part, got = folded
    mid, to_right, to_left, new, part = call(
        stage_four_kernel,
        sc,
        (old, strip, first, second, power, part, got),
        ((256, 256), (256, 256), (256, 128), (448, 256), (264, PR)),
    )
    lft, rgt, got = shift(to_right, 1), shift(to_left, -1), pair(part, 2, False)
    total = call(finish_sum_kernel, sc, (part, got), ((256, PR),), after=(lft, rgt))[0]
    aa = call(widen_kernel, sc, (lft, mid, rgt), ((256, PR),), after=(total,))[0]
    ab = swap_plane(aa)
    pieces = (aa, ab, swap_core(aa), swap_core(ab))
    mine, theirs = call(
        collect_kernel, sc, spread(total), ((PR, PR), (PR, PR)), limit=8, flops=EARLY
    )
    return pieces, (mine, swap_core(theirs)), new


def last_update(sc, p, old, folded, power):
    strip, first, second, part, got = folded
    aa, part = call(
        last_four_kernel,
        sc,
        (old, strip, first, second, power, part, got),
        ((256, 256), (264, PR)),
    )
    got = pair(part, 2, True)
    ab = swap_plane(aa)
    mine, theirs = call(
        last_sum_kernel, sc, (part, got, p), ((128, PR), (128, PR)), after=(ab,)
    )
    pieces = (aa, ab, swap_core(aa), swap_core(ab))
    field, token = call(join_field_kernel, sc, pieces, ((2, 512, 256), (8, 128)))
    other = call(last_step_kernel, sc, (p, swap_core(theirs)), ((128, PR),))[0]
    parts = [mine] + [ring(mine, d) for d in (1, 2, 3)]
    parts += [other] + [other_ring(other, d) for d in (1, 2, 3)]
    return field, call(join_probe_kernel, sc, parts, (FIELD,), limit=8, after=(token,))[0]


def body(object_field, probe, amplitudes, positions, owned):
    ty, tx, mode = lax.axis_index("ty"), lax.axis_index("tx"), lax.axis_index("mode")
    tile = ty * 8 + tx
    tiles = positions[:, 0] // 512 * 8 + positions[:, 1] // 256
    row_blocks = positions[:, 0] % 512 // 128
    col_blocks = positions[:, 1] % 256 // 128

    def pick(values, which):
        return jnp.sum(jnp.where(tiles == which, values, 0))

    core = mode % 2
    sc = jnp.stack(
        [
            pick(row_blocks, tile),
            pick(col_blocks, tile),
            pick(row_blocks, tile - 1),
            pick(row_blocks, tile + 1),
            tx % 4,
            ty,
            tx // 4,
            mode // 2,
            core,
        ]
    ).astype(jnp.int32)
    tabs = [jnp.asarray(t) for t in tables()]
    p = probe[:, 0]
    amp = call(order_kernel, sc, (amplitudes[0],), ((HALF, PR),), limit=24)[0]

    plane = lax.dynamic_index_in_dim(object_field, core, 0, keepdims=False)
    up, down = step(plane[256:512], "ty", 1), step(plane[0:128], "ty", -1)
    mid, to_right, to_left, strip = call(
        first_strips_kernel,
        sc,
        (up, plane, down),
        ((512, 256), (512, 256), (512, 128), (448, 256)),
        scratch=((896, 256),),
        limit=8,
    )
    lft, rgt = step(to_right, "tx", 1), step(to_left, "tx", -1)
    mine = call(widen_kernel, sc, (lft, mid, rgt), ((PR, PR),))[0]

    w, first = forward_first(sc, mine, swap_core(mine), p, tabs)
    *fields, power = measured_fields(sc, amp, first, tabs)
    folded = fold_gradients(sc, w, p, fields, tabs, False)
    pieces, parts, strip = update(sc, strip, folded, power)

    w, p, first = forward_second(sc, pieces, p, parts, tabs)
    *fields, power = measured_fields(sc, amp, first, tabs)
    folded = fold_gradients(sc, w, p, fields, tabs, True)
    out_field, out_probe = last_update(sc, p, strip, folded, power)
    return out_field, out_probe[:, None]


def solution(mesh):
    placed = (
        P(None, "ty", "tx"),
        P(None, "mode", None, None),
        P(("ty", "tx"), None, None),
        P(),
        P(("ty", "tx"), None),
    )
    return jax.shard_map(
        body,
        mesh=mesh,
        in_specs=placed,
        out_specs=(P(None, "ty", "tx"), P(None, "mode", None, None)),
        check_vma=False,
    )
```

```python
import functools

import jax
import jax.numpy as jnp
import numpy as np
from jax import lax
from jax.experimental import pallas as pl
from jax.experimental.pallas import tpu as pltpu
from jax.sharding import PartitionSpec as P

PR = 512
HALF = 256
F32 = jnp.float32
BF16 = jnp.bfloat16
MIB = 1 << 20

ROW, COL, ROW_LEFT, ROW_RIGHT, X, Z, YL, YH, CORE = range(9)


def split_np(matrix):
    high = matrix.astype(jnp.bfloat16)
    low = (matrix - high.astype(np.float64)).astype(jnp.bfloat16)
    return high, low


def tables():
    k = np.arange(HALF)[:, None]
    u = np.arange(HALF)[None, :]
    out = []
    for odd in (0, 1):
        angle = 2.0 * np.pi * (((2 * k + odd) * u) % PR) / PR
        c, s = np.cos(angle) / np.sqrt(PR), np.sin(angle) / np.sqrt(PR)
        out.append(np.block([[c, s], [-s, c]]))
    even, odd = out
    parts = []
    for m in (even, odd, even.T, odd.T):
        parts.extend(split_np(np.ascontiguousarray(m)))
    return parts


def split(x):
    high = x.astype(BF16)
    return high, (x - high.astype(F32)).astype(BF16)


def dot(a, b):
    return jnp.dot(a, b, preferred_element_type=F32)


def left(mh, ml, x):
    xh, xl = split(x)
    return dot(mh[...], xh) + (dot(mh[...], xl) + dot(ml[...], xh))


def right(x, mh, ml):
    xh, xl = split(x)
    return dot(xh, mh[...]) + (dot(xl, mh[...]) + dot(xh, ml[...]))


def right_t(x, mh, ml):
    def dot_t(a, b):
        return lax.dot_general(a, b, (((1,), (1,)), ((), ())), preferred_element_type=F32)

    xh, xl = split(x)
    return dot_t(xh, mh[...]) + (dot_t(xl, mh[...]) + dot_t(xh, ml[...]))


def smem():
    return pl.BlockSpec(memory_space=pltpu.SMEM)


def vmem():
    return pl.BlockSpec(memory_space=pltpu.VMEM)


def even_row(sc):
    return lax.rem(sc[Z], 2) == 0


def row_sides(sc, got_first, got_second):
    even = even_row(sc)
    return jnp.where(even, got_second, got_first), jnp.where(even, got_first, got_second)


def row_sends(sc, to_up, to_down, first, second):
    @pl.when(even_row(sc))
    def _():
        first[...] = to_down
        second[...] = to_up

    @pl.when(jnp.logical_not(even_row(sc)))
    def _():
        first[...] = to_up
        second[...] = to_down


def call(kernel, sc, ins, outs, scratch=(), limit=6, flops=0, after=()):
    count = len(ins)

    def run(sc_ref, *refs):
        kernel(sc_ref, *refs[:count], *refs[count + len(after) :])

    return pl.pallas_call(
        run,
        out_shape=[jax.ShapeDtypeStruct(s, F32) for s in outs],
        in_specs=[smem()] + [vmem()] * count + [pl.BlockSpec(memory_space=pl.ANY)] * len(after),
        out_specs=[vmem()] * len(outs),
        scratch_shapes=[pltpu.VMEM(s, F32) for s in scratch],
        compiler_params=pltpu.CompilerParams(vmem_limit_bytes=limit * MIB),
        cost_estimate=pl.CostEstimate(
            flops=flops,
            bytes_accessed=4 * sum(int(np.prod(s)) for s in outs) + sum(a.nbytes for a in ins),
            transcendentals=0,
        ),
    )(sc, *ins, *after)


def at(start, size, unit):
    return pl.ds(pl.multiple_of(start * unit, unit), size)


def exact_parts(x):
    a = x.astype(BF16)
    rest = x - a.astype(F32)
    b = rest.astype(BF16)
    return a, b, (rest - b.astype(F32)).astype(BF16)


def order_kernel(sc, amp, out):
    core = sc[CORE]
    row = lax.broadcasted_iota(jnp.int32, (HALF, PR), 0)
    col = lax.broadcasted_iota(jnp.int32, (HALF, PR), 1)
    pick = jnp.where(col == 2 * row + core, 1.0, 0.0).astype(BF16)
    a, b, c = exact_parts(amp[...])
    rows = (dot(pick, a) + dot(pick, b)) + dot(pick, c)
    src = lax.broadcasted_iota(jnp.int32, (PR, PR), 0)
    dst = lax.broadcasted_iota(jnp.int32, (PR, PR), 1)
    want = jnp.where(dst < HALF, 2 * dst, 2 * (dst - HALF) + 1)
    move = jnp.where(src == want, 1.0, 0.0).astype(BF16)
    a, b, c = exact_parts(rows)
    out[...] = (dot(a, move) + dot(b, move)) + dot(c, move)


def first_strips_kernel(sc, up, own, down, mid, to_right, to_left, kept, strip):
    strip[0:256] = up[...]
    strip[256:768] = own[...]
    strip[768:896] = down[...]
    mid[...] = strip[at(sc[ROW], 512, 128)]
    to_right[...] = strip[at(sc[ROW_RIGHT], 512, 128)]
    to_left[...] = strip[at(sc[ROW_LEFT], 512, 128), 0:128]
    for block in range(7):
        kept[block * 64 : block * 64 + 64] = strip[at(2 * block + sc[YH], 64, 64)]


def widen_kernel(sc, lft, mid, rgt, out):
    column = 4 * sc[YL] + sc[X]

    @pl.when(sc[COL] == 0)
    def _():
        out[:, 0:256] = jnp.where(column == 0, 0.0, lft[...])
        out[:, 256:512] = mid[...]

    @pl.when(sc[COL] != 0)
    def _():
        out[:, 0:128] = jnp.where(column == 0, 0.0, lft[:, 128:256])
        out[:, 128:384] = mid[...]
        out[:, 384:512] = jnp.where(column == 7, 0.0, rgt[...])


def left_side(w, p, tabs, mid):
    meh, mel, moh, mol = tabs
    wr, wi = w[0], w[1]
    pr, pi = p[0], p[1]
    er = pr * wr - pi * wi
    ei = pr * wi + pi * wr
    total = jnp.concatenate([er[:HALF] + er[HALF:], ei[:HALF] + ei[HALF:]], axis=0)
    mid[0] = left(meh, mel, total)
    total = jnp.concatenate([er[:HALF] - er[HALF:], ei[:HALF] - ei[HALF:]], axis=0)
    mid[1] = left(moh, mol, total)
    return (jnp.sum(pr * pr) + jnp.sum(pi * pi)) * (1.0 / (PR * PR))


def right_side(mid, parity, tabs, far, intensity):
    meh, mel, moh, mol = tabs
    yr, yi = mid[parity, 0:HALF], mid[parity, HALF:PR]
    total = jnp.concatenate([yr[:, :HALF] + yr[:, HALF:], yi[:, :HALF] + yi[:, HALF:]], axis=1)
    even = right_t(total, meh, mel)
    total = jnp.concatenate([yr[:, :HALF] - yr[:, HALF:], yi[:, :HALF] - yi[:, HALF:]], axis=1)
    odd = right_t(total, moh, mol)
    fr = jnp.concatenate([even[:, :HALF], odd[:, :HALF]], axis=1)
    fi = jnp.concatenate([even[:, HALF:], odd[:, HALF:]], axis=1)
    far[0] = fr
    far[1] = fi
    intensity[0:HALF] = fr * fr + fi * fi


def forward_tail(sc, w, p, tabs, mid, far, send, power):
    mean = left_side(w, p, tabs, mid)
    right_side(mid, 1 - sc[CORE], tabs, far, send)
    send[HALF : HALF + 8] = jnp.full((8, PR), mean, F32)
    power[...] = jnp.full((8, PR), mean, F32)


def forward_rest_kernel(sc, mid, power, *rest):
    tabs, (far, keep) = rest[:4], rest[4:]
    right_side(mid, sc[CORE], tabs, far, keep)
    keep[HALF : HALF + 8] = power[...]


def forward_first_kernel(sc, mine, other, p, *rest):
    tabs, (w, mid, far, send, power) = rest[:4], rest[4:]
    core = sc[CORE]
    w[core] = mine[...]
    w[1 - core] = other[...]
    forward_tail(sc, w, p, tabs, mid, far, send, power)


def forward_second_kernel(sc, aa, ab, ba, bb, old, mine, got, *rest):
    tabs, (w, p, mid, far, send, power) = rest[:4], rest[4:]
    core, yh = sc[CORE], sc[YH]
    for plane, parity, piece in (
        (core, yh, aa),
        (core, 1 - yh, ab),
        (1 - core, yh, ba),
        (1 - core, 1 - yh, bb),
    ):
        for block in range(4):
            w[plane, at(2 * block + parity, 64, 64)] = piece[block * 64 : block * 64 + 64]
    p[core] = old[core] - mine[...]
    p[1 - core] = old[1 - core] - got[...]
    forward_tail(sc, w, p, tabs, mid, far, send, power)


FLOPS = 3 * 8 * PR**3
FIELD = (2, PR, PR)
EXT = (HALF + 8, PR)


FIRST = (FIELD, (2, HALF, PR), EXT, (8, PR))


def forward_first(sc, mine, other, p, tabs):
    outs = call(
        forward_first_kernel,
        sc,
        (mine, other, p, *tabs[:4]),
        (FIELD,) + FIRST,
        limit=24,
        flops=FLOPS * 3 // 4,
    )
    return outs[0], outs[1:]


def forward_second(sc, pieces, p, parts, tabs):
    outs = call(
        forward_second_kernel,
        sc,
        (*pieces, p, *parts, *tabs[:4]),
        (FIELD, FIELD) + FIRST,
        limit=24,
        flops=FLOPS * 3 // 4,
    )
    return outs[0], outs[1], outs[2:]


def measured_fields(sc, amp, first, tabs):
    mid, far_send, send, power = first
    got = swap_core(send)
    far_keep, keep = call(
        forward_rest_kernel,
        sc,
        (mid, power, *tabs[:4]),
        ((2, HALF, PR), EXT),
        limit=16,
        flops=FLOPS // 4,
    )
    half = keep + got
    total = half + swap_plane(half)
    mine = 1.0 - amp / jnp.maximum(jnp.sqrt(total[:HALF]), 1.0)
    other = swap_core(mine)
    back = call(
        inverse_rows_kernel,
        sc,
        (far_keep, mine, *tabs[:4]),
        ((PR, PR),),
        limit=16,
        flops=FLOPS // 4,
    )[0]
    return back, far_send, other, total[HALF:]


def inverse_rows(far, weight, tabs):
    meh, mel, moh, mol = tabs
    yr = far[0] * weight[...]
    yi = far[1] * weight[...]
    even = right(jnp.concatenate([yr[:, :HALF], yi[:, :HALF]], axis=1), meh, mel)
    odd = right(jnp.concatenate([yr[:, HALF:], yi[:, HALF:]], axis=1), moh, mol)
    total = even + odd
    diff = even - odd
    real = jnp.concatenate([total[:, :HALF], diff[:, :HALF]], axis=1)
    return real, jnp.concatenate([total[:, HALF:], diff[:, HALF:]], axis=1)


def inverse_rows_kernel(sc, far, weight, *rest):
    tabs, out = rest[:4], rest[4]
    out[0:HALF], out[HALF:PR] = inverse_rows(far, weight, tabs)


def inverse_kernel(sc, w, p, back, far, other, *rest):
    tabs, (keep, send, stay, go, power, mid) = rest[:8], rest[8:]
    teh, tel, toh, tol = tabs[4:]
    core = sc[CORE]
    mid[core] = back[...]
    mid[1 - core, 0:HALF], mid[1 - core, HALF:PR] = inverse_rows(far, other, tabs[:4])
    even = left(teh, tel, mid[0])
    odd = left(toh, tol, mid[1])
    squares = jnp.zeros((), F32)
    for top in (0, 1):
        rows = slice(top * HALF, top * HALF + HALF)
        both = even - odd if top else even + odd
        cr, ci = both[:HALF], both[HALF:]
        pr, pi = p[0, rows], p[1, rows]
        wr, wi = w[0, rows], w[1, rows]
        for vr, vi, own, swap in ((pr, pi, keep, send), (wr, wi, stay, go)):
            gr = vr * cr + vi * ci
            gi = vr * ci - vi * cr

            @pl.when(core == 0)
            def _():
                own[rows] = gr
                swap[rows] = gi

            @pl.when(core != 0)
            def _():
                own[rows] = gi
                swap[rows] = gr

        squares = squares + (jnp.sum(wr * wr) + jnp.sum(wi * wi))
    power[...] = jnp.full((8, PR), squares * (1.0 / (PR * PR)), F32)


def inverse(sc, w, p, back, far, other, tabs):
    return call(
        inverse_kernel,
        sc,
        (w, p, back, far, other, *tabs),
        ((PR, PR), (PR, PR), (PR, PR), (PR, PR), (8, PR)),
        scratch=(FIELD,),
        limit=24,
        flops=FLOPS * 3 // 4,
    )


def halve_kernel(sc, keep, got, stay, go):
    yh = sc[YH]
    for block in range(4):
        rows = slice(block * 64, block * 64 + 64)
        here = at(2 * block + yh, 64, 64)
        there = at(2 * block + 1 - yh, 64, 64)
        stay[rows] = keep[here] + got[here]
        go[rows] = keep[there] + got[there]


def ring_place(sc):
    return jnp.where(sc[CORE] == 0, sc[X], sc[Z])


def chunk_kernel(sc, mine, got, power, *outs):
    place, core = ring_place(sc), sc[CORE]
    for d, out in enumerate(outs):
        rows = at(lax.rem(place + d, 4), 128, 128)
        out[at(core, 128, 128)] = mine[rows]
        out[at(1 - core, 128, 128)] = got[rows]
        out[256:264] = power[...]


def fold_kernel(sc, stay, got, lft, mid, rgt):
    g = stay[...] + got[...]

    @pl.when(sc[COL] == 0)
    def _():
        lft[...] = g[:, 0:256]
        mid[...] = g[:, 256:512]
        rgt[...] = jnp.zeros(rgt.shape, F32)

    @pl.when(sc[COL] != 0)
    def _():
        lft[:, 0:128] = jnp.zeros((g.shape[0], 128), F32)
        lft[:, 128:256] = g[:, 0:128]
        mid[...] = g[:, 128:384]
        rgt[...] = g[:, 384:512]


def ring_sum_kernel(sc, c0, c1, c2, c3, total):
    total[...] = (c0[...] + c1[...]) + (c2[...] + c3[...])


def stage_three_kernel(sc, mid, from_right, from_left, part, got, strip, first, second, total):
    column = 4 * sc[YL] + sc[X]
    strip[...] = jnp.zeros(strip.shape, F32)
    strip[at(sc[ROW], 256, 64)] = mid[...]
    rows = at(sc[ROW_RIGHT], 256, 64)
    strip[rows] = strip[rows] + jnp.where(column == 7, 0.0, from_right[...])
    rows = at(sc[ROW_LEFT], 256, 64)
    strip[rows, 0:128] = strip[rows, 0:128] + jnp.where(column == 0, 0.0, from_left[...])
    row_sends(sc, strip[0:192], strip[256:448], first, second)
    total[...] = part[...] + got[...]


def stage_four_kernel(
    sc, old, strip, got_first, got_second, power, part, got,
    mid, to_right, to_left, new, total,
):
    z = sc[Z]
    from_up, from_down = row_sides(sc, got_first[...], got_second[...])
    light = 2.0 * power[0:1, 0:1]
    above = jnp.where(z == 0, 0.0, 1.0)
    below = jnp.where(z == 3, 0.0, 1.0)
    new[0:128] = (old[0:128] - (strip[0:128] + from_up[0:128]) / light) * above
    new[128:192] = old[128:192] - (strip[128:192] + from_up[128:192]) / light
    new[192:256] = old[192:256] - strip[192:256] / light
    new[256:384] = old[256:384] - (strip[256:384] + from_down[0:128]) / light
    new[384:448] = (old[384:448] - (strip[384:448] + from_down[128:192]) / light) * below
    mid[...] = new[at(sc[ROW], 256, 64)]
    to_right[...] = new[at(sc[ROW_RIGHT], 256, 64)]
    to_left[...] = new[at(sc[ROW_LEFT], 256, 64), 0:128]
    total[...] = part[...] + got[...]


def last_four_kernel(sc, old, strip, got_first, got_second, power, part, got, new, total):
    from_up, from_down = row_sides(sc, got_first[...], got_second[...])
    light = 2.0 * power[0:1, 0:1]
    new[0:64] = old[128:192] - (strip[128:192] + from_up[128:192]) / light
    new[64:128] = old[192:256] - strip[192:256] / light
    new[128:256] = old[256:384] - (strip[256:384] + from_down[0:128]) / light
    total[...] = part[...] + got[...]


def finish_sum_kernel(sc, part, got, total):
    power = part[256:257, 0:1] + got[256:257, 0:1]
    total[...] = (part[0:256] + got[0:256]) / power


def last_sum_kernel(sc, part, got, old, mine, theirs):
    core = sc[CORE]
    power = part[256:257, 0:1] + got[256:257, 0:1]
    rows = at(core, 128, 128)
    here = at(ring_place(sc), 128, 128)
    mine[...] = old[core, here] - (part[rows] + got[rows]) / power
    rows = at(1 - core, 128, 128)
    theirs[...] = (part[rows] + got[rows]) / power


def other_place(sc):
    return jnp.where(sc[CORE] == 0, sc[Z], sc[X])


def last_step_kernel(sc, old, got, out):
    out[...] = old[1 - sc[CORE], at(other_place(sc), 128, 128)] - got[...]


def collect_kernel(sc, c0, c1, c2, c3, mine, theirs):
    place, core = ring_place(sc), sc[CORE]
    for d, part in enumerate((c0, c1, c2, c3)):
        rows = at(lax.rem(place + 4 - d, 4), 128, 128)
        mine[rows] = part[at(core, 128, 128)]
        theirs[rows] = part[at(1 - core, 128, 128)]


def join_probe_kernel(sc, *refs):
    parts, out = refs[:8], refs[8]
    core = sc[CORE]
    for n, part in enumerate(parts):
        plane, place = (core, ring_place(sc)) if n < 4 else (1 - core, other_place(sc))
        out[plane, at(lax.rem(place + 4 - n % 4, 4), 128, 128)] = part[...]


def join_field_kernel(sc, aa, ab, ba, bb, out, token):
    token[...] = jnp.zeros(token.shape, F32)
    core, yh = sc[CORE], sc[YH]
    for block in range(4):
        rows = slice(block * 64, block * 64 + 64)
        out[core, at(2 * block + yh, 64, 64)] = aa[rows]
        out[core, at(2 * block + 1 - yh, 64, 64)] = ab[rows]
        out[1 - core, at(2 * block + yh, 64, 64)] = ba[rows]
        out[1 - core, at(2 * block + 1 - yh, 64, 64)] = bb[rows]


def swap_core(v):
    return lax.ppermute(v, "mode", [(0, 1), (1, 0), (2, 3), (3, 2)])


def swap_plane(v):
    return lax.ppermute(v, "mode", [(0, 2), (2, 0), (1, 3), (3, 1)])


def permute(v, move):
    pairs = []
    for z in range(4):
        for y in range(2):
            for x in range(4):
                for mode in range(4):
                    tx, ty, tz = move(mode % 2, x, y, z)
                    pairs.append((((z * 2 + y) * 4 + x) * 4 + mode, ((tz * 2 + ty) * 4 + tx) * 4 + mode))
    return lax.ppermute(v, ("ty", "tx", "mode"), pairs)


def ring(v, d):
    return permute(v, lambda core, x, y, z: (x, y, (z + d) % 4) if core else ((x + d) % 4, y, z))


def other_ring(v, d):
    return permute(v, lambda core, x, y, z: ((x + d) % 4, y, z) if core else (x, y, (z + d) % 4))


def pair(v, turn, last):
    def move(core, x, y, z):
        if core == 0:
            return x, 1 - y if turn == 1 else y, (z ^ 1, z, 3 - z)[turn]
        x_turn = turn - 1 if last else turn
        if x_turn in (0, 1):
            return (x ^ 1, 3 - x)[x_turn], y, z
        return x, 1 - y, z

    return permute(v, move)


def step(v, axis, d):
    count = {"ty": 4, "tx": 8}[axis]
    return lax.ppermute(v, axis, [(i, i + d) for i in range(count) if 0 <= i + d < count])


def shift(v, d):
    return lax.ppermute(v, "tx", [(i, (i + d) % 8) for i in range(8)])


def swap_rows(first, second):
    return (
        lax.ppermute(first, "ty", [(0, 1), (1, 0), (2, 3), (3, 2)]),
        lax.ppermute(second, "ty", [(1, 2), (2, 1)]),
    )


EARLY = 6 * 10**9


def fold_gradients(sc, w, p, fields, tabs, last):
    keep, send, mine, theirs, window_power = inverse(sc, w, p, *fields, tabs)
    got = swap_core(send)
    other = swap_core(theirs)
    chunks = call(chunk_kernel, sc, (mine, other, window_power), ((264, PR),) * 4, limit=8)
    stay, go = call(
        halve_kernel, sc, (keep, got), ((HALF, PR), (HALF, PR)), limit=8, after=(chunks[0],)
    )
    got = swap_plane(go)
    chunks = [chunks[0]] + [ring(chunks[d], d) for d in (1, 2, 3)]
    part = call(ring_sum_kernel, sc, chunks, ((264, PR),), flops=EARLY)[0]
    lft, mid, rgt = call(
        fold_kernel, sc, (stay, got), ((HALF, 256), (HALF, 256), (HALF, 128)), limit=8, after=(part,)
    )
    from_right, from_left, got = shift(lft, -1), shift(rgt, 1), pair(part, 0, last)
    strip, first, second, part = call(
        stage_three_kernel,
        sc,
        (mid, from_right, from_left, part, got),
        ((448, 256), (192, 256), (192, 256), (264, PR)),
    )
    first, second = swap_rows(first, second)
    return strip, first, second, part, pair(part, 1, last)


def spread(total):
    return total, ring(total, 1), ring(total, 2), ring(total, 3)


def update(sc, old, folded, power):
    strip, first, second, part, got = folded
    mid, to_right, to_left, new, part = call(
        stage_four_kernel,
        sc,
        (old, strip, first, second, power, part, got),
        ((256, 256), (256, 256), (256, 128), (448, 256), (264, PR)),
    )
    lft, rgt, got = shift(to_right, 1), shift(to_left, -1), pair(part, 2, False)
    total = call(finish_sum_kernel, sc, (part, got), ((256, PR),), after=(lft, rgt))[0]
    aa = call(widen_kernel, sc, (lft, mid, rgt), ((256, PR),), after=(total,))[0]
    ab = swap_plane(aa)
    pieces = (aa, ab, swap_core(aa), swap_core(ab))
    mine, theirs = call(
        collect_kernel, sc, spread(total), ((PR, PR), (PR, PR)), limit=8, flops=EARLY
    )
    return pieces, (mine, swap_core(theirs)), new


def last_update(sc, p, old, folded, power):
    strip, first, second, part, got = folded
    aa, part = call(
        last_four_kernel,
        sc,
        (old, strip, first, second, power, part, got),
        ((256, 256), (264, PR)),
    )
    got = pair(part, 2, True)
    ab = swap_plane(aa)
    mine, theirs = call(
        last_sum_kernel, sc, (part, got, p), ((128, PR), (128, PR)), after=(ab,)
    )
    pieces = (aa, ab, swap_core(aa), swap_core(ab))
    field, token = call(join_field_kernel, sc, pieces, ((2, 512, 256), (8, 128)))
    other = call(last_step_kernel, sc, (p, swap_core(theirs)), ((128, PR),))[0]
    parts = [mine] + [ring(mine, d) for d in (1, 2, 3)]
    parts += [other] + [other_ring(other, d) for d in (1, 2, 3)]
    return field, call(join_probe_kernel, sc, parts, (FIELD,), limit=8, after=(token,))[0]


def body(object_field, probe, amplitudes, positions, owned):
    ty, tx, mode = lax.axis_index("ty"), lax.axis_index("tx"), lax.axis_index("mode")
    tile = ty * 8 + tx
    tiles = positions[:, 0] // 512 * 8 + positions[:, 1] // 256
    row_blocks = positions[:, 0] % 512 // 128
    col_blocks = positions[:, 1] % 256 // 128

    def pick(values, which):
        return jnp.sum(jnp.where(tiles == which, values, 0))

    core = mode % 2
    sc = jnp.stack(
        [
            pick(row_blocks, tile),
            pick(col_blocks, tile),
            pick(row_blocks, tile - 1),
            pick(row_blocks, tile + 1),
            tx % 4,
            ty,
            tx // 4,
            mode // 2,
            core,
        ]
    ).astype(jnp.int32)
    tabs = [jnp.asarray(t) for t in tables()]
    p = probe[:, 0]
    amp = call(order_kernel, sc, (amplitudes[0],), ((HALF, PR),), limit=24)[0]

    plane = lax.dynamic_index_in_dim(object_field, core, 0, keepdims=False)
    up, down = step(plane[256:512], "ty", 1), step(plane[0:128], "ty", -1)
    mid, to_right, to_left, strip = call(
        first_strips_kernel,
        sc,
        (up, plane, down),
        ((512, 256), (512, 256), (512, 128), (448, 256)),
        scratch=((896, 256),),
        limit=8,
    )
    lft, rgt = step(to_right, "tx", 1), step(to_left, "tx", -1)
    mine = call(widen_kernel, sc, (lft, mid, rgt), ((PR, PR),))[0]

    w, first = forward_first(sc, mine, swap_core(mine), p, tabs)
    *fields, power = measured_fields(sc, amp, first, tabs)
    folded = fold_gradients(sc, w, p, fields, tabs, False)
    pieces, parts, strip = update(sc, strip, folded, power)

    w, p, first = forward_second(sc, pieces, p, parts, tabs)
    *fields, power = measured_fields(sc, amp, first, tabs)
    folded = fold_gradients(sc, w, p, fields, tabs, True)
    out_field, out_probe = last_update(sc, p, strip, folded, power)
    return out_field, out_probe[:, None]


def solution(mesh):
    placed = (
        P(None, "ty", "tx"),
        P(None, "mode", None, None),
        P(("ty", "tx"), None, None),
        P(),
        P(("ty", "tx"), None),
    )
    return jax.shard_map(
        body,
        mesh=mesh,
        in_specs=placed,
        out_specs=(P(None, "ty", "tx"), P(None, "mode", None, None)),
        check_vma=False,
    )
```

```python
import functools

import jax
import jax.numpy as jnp
import numpy as np
from jax import lax
from jax.experimental import pallas as pl
from jax.experimental.pallas import tpu as pltpu
from jax.sharding import PartitionSpec as P

PR = 512
HALF = 256
F32 = jnp.float32
BF16 = jnp.bfloat16
MIB = 1 << 20

ROW, COL, ROW_LEFT, ROW_RIGHT, X, Z, YL, YH, CORE = range(9)


def split_np(matrix):
    high = matrix.astype(jnp.bfloat16)
    low = (matrix - high.astype(np.float64)).astype(jnp.bfloat16)
    return high, low


def tables():
    k = np.arange(HALF)[:, None]
    u = np.arange(HALF)[None, :]
    out = []
    for odd in (0, 1):
        angle = 2.0 * np.pi * (((2 * k + odd) * u) % PR) / PR
        c, s = np.cos(angle) / np.sqrt(PR), np.sin(angle) / np.sqrt(PR)
        out.append(np.block([[c, s], [-s, c]]))
    even, odd = out
    parts = []
    for m in (even, odd, even.T, odd.T):
        parts.extend(split_np(np.ascontiguousarray(m)))
    return parts


def split(x):
    high = x.astype(BF16)
    return high, (x - high.astype(F32)).astype(BF16)


def dot(a, b):
    return jnp.dot(a, b, preferred_element_type=F32)


def left(mh, ml, x):
    xh, xl = split(x)
    return dot(mh[...], xh) + (dot(mh[...], xl) + dot(ml[...], xh))


def right(x, mh, ml):
    xh, xl = split(x)
    return dot(xh, mh[...]) + (dot(xl, mh[...]) + dot(xh, ml[...]))


def right_t(x, mh, ml):
    def dot_t(a, b):
        return lax.dot_general(a, b, (((1,), (1,)), ((), ())), preferred_element_type=F32)

    xh, xl = split(x)
    return dot_t(xh, mh[...]) + (dot_t(xl, mh[...]) + dot_t(xh, ml[...]))


def smem():
    return pl.BlockSpec(memory_space=pltpu.SMEM)


def vmem():
    return pl.BlockSpec(memory_space=pltpu.VMEM)


def even_row(sc):
    return lax.rem(sc[Z], 2) == 0


def row_sides(sc, got_first, got_second):
    even = even_row(sc)
    return jnp.where(even, got_second, got_first), jnp.where(even, got_first, got_second)


def row_sends(sc, to_up, to_down, first, second):
    @pl.when(even_row(sc))
    def _():
        first[...] = to_down
        second[...] = to_up

    @pl.when(jnp.logical_not(even_row(sc)))
    def _():
        first[...] = to_up
        second[...] = to_down


def call(kernel, sc, ins, outs, scratch=(), limit=6, flops=0, after=()):
    count = len(ins)

    def run(sc_ref, *refs):
        kernel(sc_ref, *refs[:count], *refs[count + len(after) :])

    return pl.pallas_call(
        run,
        out_shape=[jax.ShapeDtypeStruct(s, F32) for s in outs],
        in_specs=[smem()] + [vmem()] * count + [pl.BlockSpec(memory_space=pl.ANY)] * len(after),
        out_specs=[vmem()] * len(outs),
        scratch_shapes=[pltpu.VMEM(s, F32) for s in scratch],
        compiler_params=pltpu.CompilerParams(vmem_limit_bytes=limit * MIB),
        cost_estimate=pl.CostEstimate(
            flops=flops,
            bytes_accessed=4 * sum(int(np.prod(s)) for s in outs) + sum(a.nbytes for a in ins),
            transcendentals=0,
        ),
    )(sc, *ins, *after)


def at(start, size, unit):
    return pl.ds(pl.multiple_of(start * unit, unit), size)


def exact_parts(x):
    a = x.astype(BF16)
    rest = x - a.astype(F32)
    b = rest.astype(BF16)
    return a, b, (rest - b.astype(F32)).astype(BF16)


def order_kernel(sc, amp, out):
    core = sc[CORE]
    row = lax.broadcasted_iota(jnp.int32, (HALF, PR), 0)
    col = lax.broadcasted_iota(jnp.int32, (HALF, PR), 1)
    pick = jnp.where(col == 2 * row + core, 1.0, 0.0).astype(BF16)
    a, b, c = exact_parts(amp[...])
    rows = (dot(pick, a) + dot(pick, b)) + dot(pick, c)
    src = lax.broadcasted_iota(jnp.int32, (PR, PR), 0)
    dst = lax.broadcasted_iota(jnp.int32, (PR, PR), 1)
    want = jnp.where(dst < HALF, 2 * dst, 2 * (dst - HALF) + 1)
    move = jnp.where(src == want, 1.0, 0.0).astype(BF16)
    a, b, c = exact_parts(rows)
    out[...] = (dot(a, move) + dot(b, move)) + dot(c, move)


def first_strips_kernel(sc, up, own, down, mid, to_right, to_left, kept, strip):
    strip[0:256] = up[...]
    strip[256:768] = own[...]
    strip[768:896] = down[...]
    mid[...] = strip[at(sc[ROW], 512, 128)]
    to_right[...] = strip[at(sc[ROW_RIGHT], 512, 128)]
    to_left[...] = strip[at(sc[ROW_LEFT], 512, 128), 0:128]
    for block in range(7):
        kept[block * 64 : block * 64 + 64] = strip[at(2 * block + sc[YH], 64, 64)]


def widen_kernel(sc, lft, mid, rgt, out):
    column = 4 * sc[YL] + sc[X]

    @pl.when(sc[COL] == 0)
    def _():
        out[:, 0:256] = jnp.where(column == 0, 0.0, lft[...])
        out[:, 256:512] = mid[...]

    @pl.when(sc[COL] != 0)
    def _():
        out[:, 0:128] = jnp.where(column == 0, 0.0, lft[:, 128:256])
        out[:, 128:384] = mid[...]
        out[:, 384:512] = jnp.where(column == 7, 0.0, rgt[...])


def left_side(w, p, tabs, mid):
    meh, mel, moh, mol = tabs
    wr, wi = w[0], w[1]
    pr, pi = p[0], p[1]
    er = pr * wr - pi * wi
    ei = pr * wi + pi * wr
    total = jnp.concatenate([er[:HALF] + er[HALF:], ei[:HALF] + ei[HALF:]], axis=0)
    mid[0] = left(meh, mel, total)
    total = jnp.concatenate([er[:HALF] - er[HALF:], ei[:HALF] - ei[HALF:]], axis=0)
    mid[1] = left(moh, mol, total)
    return (jnp.sum(pr * pr) + jnp.sum(pi * pi)) * (1.0 / (PR * PR))


def right_side(mid, parity, tabs, far, intensity):
    meh, mel, moh, mol = tabs
    yr, yi = mid[parity, 0:HALF], mid[parity, HALF:PR]
    total = jnp.concatenate([yr[:, :HALF] + yr[:, HALF:], yi[:, :HALF] + yi[:, HALF:]], axis=1)
    even = right_t(total, meh, mel)
    total = jnp.concatenate([yr[:, :HALF] - yr[:, HALF:], yi[:, :HALF] - yi[:, HALF:]], axis=1)
    odd = right_t(total, moh, mol)
    fr = jnp.concatenate([even[:, :HALF], odd[:, :HALF]], axis=1)
    fi = jnp.concatenate([even[:, HALF:], odd[:, HALF:]], axis=1)
    far[0] = fr
    far[1] = fi
    intensity[0:HALF] = fr * fr + fi * fi


def forward_tail(sc, w, p, tabs, mid, far, send, power):
    mean = left_side(w, p, tabs, mid)
    right_side(mid, 1 - sc[CORE], tabs, far, send)
    send[HALF : HALF + 8] = jnp.full((8, PR), mean, F32)
    power[...] = jnp.full((8, PR), mean, F32)


def forward_rest_kernel(sc, mid, power, w, *rest):
    tabs, (far, keep, mean) = rest[:4], rest[4:]
    squares = jnp.sum(w[0] * w[0]) + jnp.sum(w[1] * w[1])
    mean[...] = jnp.full((8, PR), squares * (1.0 / (PR * PR)), F32)
    right_side(mid, sc[CORE], tabs, far, keep)
    keep[HALF : HALF + 8] = power[...]


def forward_first_kernel(sc, mine, other, p, *rest):
    tabs, (w, mid, far, send, power) = rest[:4], rest[4:]
    core = sc[CORE]
    w[core] = mine[...]
    w[1 - core] = other[...]
    forward_tail(sc, w, p, tabs, mid, far, send, power)


def forward_second_kernel(sc, aa, ab, ba, bb, old, mine, got, *rest):
    tabs, (w, p, mid, far, send, power) = rest[:4], rest[4:]
    core, yh = sc[CORE], sc[YH]
    for plane, parity, piece in (
        (core, yh, aa),
        (core, 1 - yh, ab),
        (1 - core, yh, ba),
        (1 - core, 1 - yh, bb),
    ):
        for block in range(4):
            w[plane, at(2 * block + parity, 64, 64)] = piece[block * 64 : block * 64 + 64]
    p[core] = old[core] - mine[...]
    p[1 - core] = old[1 - core] - got[...]
    forward_tail(sc, w, p, tabs, mid, far, send, power)


FLOPS = 3 * 8 * PR**3
FIELD = (2, PR, PR)
EXT = (HALF + 8, PR)


FIRST = (FIELD, (2, HALF, PR), EXT, (8, PR))


def forward_first(sc, mine, other, p, tabs):
    outs = call(
        forward_first_kernel,
        sc,
        (mine, other, p, *tabs[:4]),
        (FIELD,) + FIRST,
        limit=24,
        flops=FLOPS * 3 // 4,
    )
    return outs[0], outs[1:]


def forward_second(sc, pieces, p, parts, tabs):
    outs = call(
        forward_second_kernel,
        sc,
        (*pieces, p, *parts, *tabs[:4]),
        (FIELD, FIELD) + FIRST,
        limit=24,
        flops=FLOPS * 3 // 4,
    )
    return outs[0], outs[1], outs[2:]


def measured_fields(sc, amp, w, first, tabs):
    mid, far_send, send, power = first
    got = swap_core(send)
    far_keep, keep, window_power = call(
        forward_rest_kernel,
        sc,
        (mid, power, w, *tabs[:4]),
        ((2, HALF, PR), EXT, (8, PR)),
        limit=16,
        flops=FLOPS // 4,
    )
    half = keep + got
    total = half + swap_plane(half)
    mine = 1.0 - amp / jnp.maximum(jnp.sqrt(total[:HALF]), 1.0)
    other = swap_core(mine)
    back = call(
        inverse_rows_kernel,
        sc,
        (far_keep, mine, *tabs[:4]),
        ((PR, PR),),
        limit=16,
        flops=FLOPS // 4,
    )[0]
    return back, far_send, other, window_power, total[HALF:]


def inverse_rows(far, weight, tabs):
    meh, mel, moh, mol = tabs
    yr = far[0] * weight[...]
    yi = far[1] * weight[...]
    even = right(jnp.concatenate([yr[:, :HALF], yi[:, :HALF]], axis=1), meh, mel)
    odd = right(jnp.concatenate([yr[:, HALF:], yi[:, HALF:]], axis=1), moh, mol)
    total = even + odd
    diff = even - odd
    real = jnp.concatenate([total[:, :HALF], diff[:, :HALF]], axis=1)
    return real, jnp.concatenate([total[:, HALF:], diff[:, HALF:]], axis=1)


def inverse_rows_kernel(sc, far, weight, *rest):
    tabs, out = rest[:4], rest[4]
    out[0:HALF], out[HALF:PR] = inverse_rows(far, weight, tabs)


def inverse_kernel(sc, w, p, back, far, other, *rest):
    tabs, (keep, send, stay, go, mid) = rest[:8], rest[8:]
    teh, tel, toh, tol = tabs[4:]
    core = sc[CORE]
    mid[core] = back[...]
    mid[1 - core, 0:HALF], mid[1 - core, HALF:PR] = inverse_rows(far, other, tabs[:4])
    even = left(teh, tel, mid[0])
    odd = left(toh, tol, mid[1])
    for top in (0, 1):
        rows = slice(top * HALF, top * HALF + HALF)
        both = even - odd if top else even + odd
        cr, ci = both[:HALF], both[HALF:]
        pr, pi = p[0, rows], p[1, rows]
        wr, wi = w[0, rows], w[1, rows]
        for vr, vi, own, swap in ((pr, pi, keep, send), (wr, wi, stay, go)):
            gr = vr * cr + vi * ci
            gi = vr * ci - vi * cr

            @pl.when(core == 0)
            def _():
                own[rows] = gr
                swap[rows] = gi

            @pl.when(core != 0)
            def _():
                own[rows] = gi
                swap[rows] = gr


def inverse(sc, w, p, back, far, other, tabs):
    return call(
        inverse_kernel,
        sc,
        (w, p, back, far, other, *tabs),
        ((PR, PR), (PR, PR), (PR, PR), (PR, PR)),
        scratch=(FIELD,),
        limit=24,
        flops=FLOPS * 3 // 4,
    )


def halve_kernel(sc, keep, got, stay, go):
    yh = sc[YH]
    for block in range(4):
        rows = slice(block * 64, block * 64 + 64)
        here = at(2 * block + yh, 64, 64)
        there = at(2 * block + 1 - yh, 64, 64)
        stay[rows] = keep[here] + got[here]
        go[rows] = keep[there] + got[there]


def ring_place(sc):
    return jnp.where(sc[CORE] == 0, sc[X], sc[Z])


def chunk_kernel(sc, mine, got, power, *outs):
    place, core = ring_place(sc), sc[CORE]
    for d, out in enumerate(outs):
        rows = at(lax.rem(place + d, 4), 128, 128)
        out[at(core, 128, 128)] = mine[rows]
        out[at(1 - core, 128, 128)] = got[rows]
        out[256:264] = power[...]


def fold_kernel(sc, stay, got, lft, mid, rgt):
    g = stay[...] + got[...]

    @pl.when(sc[COL] == 0)
    def _():
        lft[...] = g[:, 0:256]
        mid[...] = g[:, 256:512]
        rgt[...] = jnp.zeros(rgt.shape, F32)

    @pl.when(sc[COL] != 0)
    def _():
        lft[:, 0:128] = jnp.zeros((g.shape[0], 128), F32)
        lft[:, 128:256] = g[:, 0:128]
        mid[...] = g[:, 128:384]
        rgt[...] = g[:, 384:512]


def ring_sum_kernel(sc, c0, c1, c2, c3, total):
    total[...] = (c0[...] + c1[...]) + (c2[...] + c3[...])


def stage_three_kernel(sc, mid, from_right, from_left, part, got, strip, first, second, total):
    column = 4 * sc[YL] + sc[X]
    strip[...] = jnp.zeros(strip.shape, F32)
    strip[at(sc[ROW], 256, 64)] = mid[...]
    rows = at(sc[ROW_RIGHT], 256, 64)
    strip[rows] = strip[rows] + jnp.where(column == 7, 0.0, from_right[...])
    rows = at(sc[ROW_LEFT], 256, 64)
    strip[rows, 0:128] = strip[rows, 0:128] + jnp.where(column == 0, 0.0, from_left[...])
    row_sends(sc, strip[0:192], strip[256:448], first, second)
    total[...] = part[...] + got[...]


def stage_four_kernel(
    sc, old, strip, got_first, got_second, power, part, got,
    mid, to_right, to_left, new, total,
):
    z = sc[Z]
    from_up, from_down = row_sides(sc, got_first[...], got_second[...])
    light = 2.0 * power[0:1, 0:1]
    above = jnp.where(z == 0, 0.0, 1.0)
    below = jnp.where(z == 3, 0.0, 1.0)
    new[0:128] = (old[0:128] - (strip[0:128] + from_up[0:128]) / light) * above
    new[128:192] = old[128:192] - (strip[128:192] + from_up[128:192]) / light
    new[192:256] = old[192:256] - strip[192:256] / light
    new[256:384] = old[256:384] - (strip[256:384] + from_down[0:128]) / light
    new[384:448] = (old[384:448] - (strip[384:448] + from_down[128:192]) / light) * below
    mid[...] = new[at(sc[ROW], 256, 64)]
    to_right[...] = new[at(sc[ROW_RIGHT], 256, 64)]
    to_left[...] = new[at(sc[ROW_LEFT], 256, 64), 0:128]
    total[...] = part[...] + got[...]


def last_four_kernel(sc, old, strip, got_first, got_second, power, part, got, new, total):
    from_up, from_down = row_sides(sc, got_first[...], got_second[...])
    light = 2.0 * power[0:1, 0:1]
    new[0:64] = old[128:192] - (strip[128:192] + from_up[128:192]) / light
    new[64:128] = old[192:256] - strip[192:256] / light
    new[128:256] = old[256:384] - (strip[256:384] + from_down[0:128]) / light
    total[...] = part[...] + got[...]


def finish_sum_kernel(sc, part, got, total):
    power = part[256:257, 0:1] + got[256:257, 0:1]
    total[...] = (part[0:256] + got[0:256]) / power


def last_sum_kernel(sc, part, got, old, mine, theirs):
    core = sc[CORE]
    power = part[256:257, 0:1] + got[256:257, 0:1]
    rows = at(core, 128, 128)
    here = at(ring_place(sc), 128, 128)
    mine[...] = old[core, here] - (part[rows] + got[rows]) / power
    rows = at(1 - core, 128, 128)
    theirs[...] = (part[rows] + got[rows]) / power


def other_place(sc):
    return jnp.where(sc[CORE] == 0, sc[Z], sc[X])


def last_step_kernel(sc, old, got, out):
    out[...] = old[1 - sc[CORE], at(other_place(sc), 128, 128)] - got[...]


def collect_kernel(sc, c0, c1, c2, c3, mine, theirs):
    place, core = ring_place(sc), sc[CORE]
    for d, part in enumerate((c0, c1, c2, c3)):
        rows = at(lax.rem(place + 4 - d, 4), 128, 128)
        mine[rows] = part[at(core, 128, 128)]
        theirs[rows] = part[at(1 - core, 128, 128)]


def join_probe_kernel(sc, *refs):
    parts, out = refs[:8], refs[8]
    core = sc[CORE]
    for n, part in enumerate(parts):
        plane, place = (core, ring_place(sc)) if n < 4 else (1 - core, other_place(sc))
        out[plane, at(lax.rem(place + 4 - n % 4, 4), 128, 128)] = part[...]


def join_field_kernel(sc, aa, ab, ba, bb, out, token):
    token[...] = jnp.zeros(token.shape, F32)
    core, yh = sc[CORE], sc[YH]
    for block in range(4):
        rows = slice(block * 64, block * 64 + 64)
        out[core, at(2 * block + yh, 64, 64)] = aa[rows]
        out[core, at(2 * block + 1 - yh, 64, 64)] = ab[rows]
        out[1 - core, at(2 * block + yh, 64, 64)] = ba[rows]
        out[1 - core, at(2 * block + 1 - yh, 64, 64)] = bb[rows]


def swap_core(v):
    return lax.ppermute(v, "mode", [(0, 1), (1, 0), (2, 3), (3, 2)])


def swap_plane(v):
    return lax.ppermute(v, "mode", [(0, 2), (2, 0), (1, 3), (3, 1)])


def permute(v, move):
    pairs = []
    for z in range(4):
        for y in range(2):
            for x in range(4):
                for mode in range(4):
                    tx, ty, tz = move(mode % 2, x, y, z)
                    pairs.append((((z * 2 + y) * 4 + x) * 4 + mode, ((tz * 2 + ty) * 4 + tx) * 4 + mode))
    return lax.ppermute(v, ("ty", "tx", "mode"), pairs)


def ring(v, d):
    return permute(v, lambda core, x, y, z: (x, y, (z + d) % 4) if core else ((x + d) % 4, y, z))


def other_ring(v, d):
    return permute(v, lambda core, x, y, z: ((x + d) % 4, y, z) if core else (x, y, (z + d) % 4))


def pair(v, turn, last):
    def move(core, x, y, z):
        if core == 0:
            return x, 1 - y if turn == 1 else y, (z ^ 1, z, 3 - z)[turn]
        x_turn = turn - 1 if last else turn
        if x_turn in (0, 1):
            return (x ^ 1, 3 - x)[x_turn], y, z
        return x, 1 - y, z

    return permute(v, move)


def step(v, axis, d):
    count = {"ty": 4, "tx": 8}[axis]
    return lax.ppermute(v, axis, [(i, i + d) for i in range(count) if 0 <= i + d < count])


def shift(v, d):
    return lax.ppermute(v, "tx", [(i, (i + d) % 8) for i in range(8)])


def swap_rows(first, second):
    return (
        lax.ppermute(first, "ty", [(0, 1), (1, 0), (2, 3), (3, 2)]),
        lax.ppermute(second, "ty", [(1, 2), (2, 1)]),
    )


EARLY = 6 * 10**9


def fold_gradients(sc, w, p, fields, window_power, tabs, last):
    keep, send, mine, theirs = inverse(sc, w, p, *fields, tabs)
    got = swap_core(send)
    other = swap_core(theirs)
    chunks = call(chunk_kernel, sc, (mine, other, window_power), ((264, PR),) * 4, limit=8)
    stay, go = call(
        halve_kernel, sc, (keep, got), ((HALF, PR), (HALF, PR)), limit=8, after=(chunks[0],)
    )
    got = swap_plane(go)
    chunks = [chunks[0]] + [ring(chunks[d], d) for d in (1, 2, 3)]
    part = call(ring_sum_kernel, sc, chunks, ((264, PR),), flops=EARLY)[0]
    lft, mid, rgt = call(
        fold_kernel, sc, (stay, got), ((HALF, 256), (HALF, 256), (HALF, 128)), limit=8, after=(part,)
    )
    from_right, from_left, got = shift(lft, -1), shift(rgt, 1), pair(part, 0, last)
    strip, first, second, part = call(
        stage_three_kernel,
        sc,
        (mid, from_right, from_left, part, got),
        ((448, 256), (192, 256), (192, 256), (264, PR)),
    )
    first, second = swap_rows(first, second)
    return strip, first, second, part, pair(part, 1, last)


def spread(total):
    return total, ring(total, 1), ring(total, 2), ring(total, 3)


def update(sc, old, folded, power):
    strip, first, second, part, got = folded
    mid, to_right, to_left, new, part = call(
        stage_four_kernel,
        sc,
        (old, strip, first, second, power, part, got),
        ((256, 256), (256, 256), (256, 128), (448, 256), (264, PR)),
    )
    lft, rgt, got = shift(to_right, 1), shift(to_left, -1), pair(part, 2, False)
    total = call(finish_sum_kernel, sc, (part, got), ((256, PR),), after=(lft, rgt))[0]
    aa = call(widen_kernel, sc, (lft, mid, rgt), ((256, PR),), after=(total,))[0]
    ab = swap_plane(aa)
    pieces = (aa, ab, swap_core(aa), swap_core(ab))
    mine, theirs = call(
        collect_kernel, sc, spread(total), ((PR, PR), (PR, PR)), limit=8, flops=EARLY
    )
    return pieces, (mine, swap_core(theirs)), new


def last_update(sc, p, old, folded, power):
    strip, first, second, part, got = folded
    aa, part = call(
        last_four_kernel,
        sc,
        (old, strip, first, second, power, part, got),
        ((256, 256), (264, PR)),
    )
    got = pair(part, 2, True)
    ab = swap_plane(aa)
    mine, theirs = call(
        last_sum_kernel, sc, (part, got, p), ((128, PR), (128, PR)), after=(ab,)
    )
    pieces = (aa, ab, swap_core(aa), swap_core(ab))
    field, token = call(join_field_kernel, sc, pieces, ((2, 512, 256), (8, 128)))
    other = call(last_step_kernel, sc, (p, swap_core(theirs)), ((128, PR),))[0]
    parts = [mine] + [ring(mine, d) for d in (1, 2, 3)]
    parts += [other] + [other_ring(other, d) for d in (1, 2, 3)]
    return field, call(join_probe_kernel, sc, parts, (FIELD,), limit=8, after=(token,))[0]


def body(object_field, probe, amplitudes, positions, owned):
    ty, tx, mode = lax.axis_index("ty"), lax.axis_index("tx"), lax.axis_index("mode")
    tile = ty * 8 + tx
    tiles = positions[:, 0] // 512 * 8 + positions[:, 1] // 256
    row_blocks = positions[:, 0] % 512 // 128
    col_blocks = positions[:, 1] % 256 // 128

    def pick(values, which):
        return jnp.sum(jnp.where(tiles == which, values, 0))

    core = mode % 2
    sc = jnp.stack(
        [
            pick(row_blocks, tile),
            pick(col_blocks, tile),
            pick(row_blocks, tile - 1),
            pick(row_blocks, tile + 1),
            tx % 4,
            ty,
            tx // 4,
            mode // 2,
            core,
        ]
    ).astype(jnp.int32)
    tabs = [jnp.asarray(t) for t in tables()]
    p = probe[:, 0]
    amp = call(order_kernel, sc, (amplitudes[0],), ((HALF, PR),), limit=24)[0]

    plane = lax.dynamic_index_in_dim(object_field, core, 0, keepdims=False)
    up, down = step(plane[256:512], "ty", 1), step(plane[0:128], "ty", -1)
    mid, to_right, to_left, strip = call(
        first_strips_kernel,
        sc,
        (up, plane, down),
        ((512, 256), (512, 256), (512, 128), (448, 256)),
        scratch=((896, 256),),
        limit=8,
    )
    lft, rgt = step(to_right, "tx", 1), step(to_left, "tx", -1)
    mine = call(widen_kernel, sc, (lft, mid, rgt), ((PR, PR),))[0]

    w, first = forward_first(sc, mine, swap_core(mine), p, tabs)
    *fields, window_power, power = measured_fields(sc, amp, w, first, tabs)
    folded = fold_gradients(sc, w, p, fields, window_power, tabs, False)
    pieces, parts, strip = update(sc, strip, folded, power)

    w, p, first = forward_second(sc, pieces, p, parts, tabs)
    *fields, window_power, power = measured_fields(sc, amp, w, first, tabs)
    folded = fold_gradients(sc, w, p, fields, window_power, tabs, True)
    out_field, out_probe = last_update(sc, p, strip, folded, power)
    return out_field, out_probe[:, None]


def solution(mesh):
    placed = (
        P(None, "ty", "tx"),
        P(None, "mode", None, None),
        P(("ty", "tx"), None, None),
        P(),
        P(("ty", "tx"), None),
    )
    return jax.shard_map(
        body,
        mesh=mesh,
        in_specs=placed,
        out_specs=(P(None, "ty", "tx"), P(None, "mode", None, None)),
        check_vma=False,
    )
```
